32 devices in a mesh: pop: 8 (over y, x, core), tp: 4 (over z).
Axes of the slice: x: 2, y: 2, z: 4, core: 2. Of those that a mesh axis runs over, the one named last changes fastest.
Arguments:
- tokens: bfloat16 [8, 256, 4096], P('pop', None, 'tp'), may hold values from -6 to 6
- receptance: bfloat16 [8, 256, 4096], P('pop', None, 'tp'), may hold values from -6 to 6
- keys: bfloat16 [8, 256, 4096], P('pop', None, 'tp'), may hold values from -0.29882812 to 0.29882812
- log_decay: bfloat16 [8, 256, 4096], P('pop', None, 'tp'), may hold values from -1 to 0
- value_weight: bfloat16 [4096, 4096], P('pop', 'tp'), may hold values from -0.09375 to 0.09375
- noise_in: bfloat16 [8, 4096], P('pop'), may hold values from -6 to 6
- noise_out: bfloat16 [8, 4096], P('pop', 'tp'), may hold values from -6 to 6
- utilities: float32 [8], P('pop'), may hold values from -0.5 to 0.5, as said below
- live_length: int32 [8], P('pop'), may hold values from 1 to 256, as said below
Outputs:
- wkv_out: bfloat16 [8, 256, 4096], P('pop', None, 'tp')
- update: float32 [4096, 4096], P('pop', 'tp')
The draws below stay inside these ranges and needn't reach their ends.
Inputs may be any that keep to these rules, and one draw needn't show every extreme that they name: `utilities`: centered ranks: the values k / 7 - 0.5, each taken once. tokens at positions from live_length on are masked.
All inputs are finite; a program needn't handle non-finite values.
Results may differ from the reference program's by a relative error of at most 0.0049.
Values may be sent and summed in bfloat16 or wider, within the bound.
A program may use at most 128 MiB of HBM per device.

```python
import math
import jax
import jax.numpy as jnp
from jax import lax

D = 4096
HEAD = 64
HEADS = 64
MEMBERS = 8
EPISODE_SYMBOLS = 256


def draw_log_decay(key, part):
    keys_list = jax.random.split(key, 5)
    channel = jax.random.uniform(keys_list[0], (D,), minval=math.log(0.002), maxval=math.log(0.06))
    member = jax.random.uniform(keys_list[1], (MEMBERS, 1, 1), minval=math.log(0.5), maxval=math.log(2.0))
    rough = jax.random.uniform(keys_list[2], (MEMBERS, EPISODE_SYMBOLS, D), minval=0.5, maxval=1.5)
    descent_multiplier = jnp.exp(channel)[None, None, :] * jnp.exp(member) * rough
    sequence_indices = jax.random.randint(keys_list[3], (MEMBERS, 3), 0, EPISODE_SYMBOLS)
    window_extent = jnp.any(jnp.arange(EPISODE_SYMBOLS)[None, :, None] == sequence_indices[:, None, :], axis=-1)
    perturb_magnitude = jax.random.uniform(keys_list[4], (MEMBERS, EPISODE_SYMBOLS, 1), minval=0.2, maxval=0.7)
    descent_multiplier = descent_multiplier + jnp.where(window_extent[:, :, None], perturb_magnitude, 0.0)
    return (-descent_multiplier).astype(jnp.bfloat16)


def draw_utilities(key, part):
    order = jax.random.permutation(key, MEMBERS)
    return order.astype(jnp.float32) / (MEMBERS - 1) - 0.5


def draw_live_length(key, part):
    keys_list = jax.random.split(key, 3)
    lengths = jax.random.randint(keys_list[0], (MEMBERS,), 1, EPISODE_SYMBOLS + 1)
    first = jax.random.randint(keys_list[1], (), 0, MEMBERS)
    second = (first + jax.random.randint(keys_list[2], (), 1, MEMBERS)) % MEMBERS
    lengths = lengths.at[first].set(EPISODE_SYMBOLS)
    lengths = lengths.at[second].set(1)
    return lengths.astype(jnp.int32)


def block_scale(stream_key, extent, cuts, smallest, high):
    def one(position, shards_of):
        steps = jax.random.uniform(jax.random.fold_in(jax.random.fold_in(stream_key, 6), position), (shards_of,), jnp.float32, smallest / len(cuts), high / len(cuts))
        return jnp.repeat(jnp.exp(steps), extent[position] // shards_of).reshape((-1,) + (1,) * (len(extent) - position - 1))

    level = one(*cuts[0])
    for cut in cuts[1:]:
        level = level * one(*cut)
    return level


def bell_draw(rng, extent, scale, most, cuts=(), held_as=jnp.bfloat16):
    array = jax.random.normal(rng, extent, jnp.float32) * scale
    if len(cuts) > 0:
        array = block_scale(rng, extent, cuts, -0.22, 0.18) * array
    return jnp.clip(array, min=-most, max=most).astype(held_as)


def setup_inputs(seed: int = 0) -> dict:
    seeds = jax.random.split(jax.random.key(seed), 10)
    return {
        "tokens": bell_draw(seeds[0], (MEMBERS, EPISODE_SYMBOLS, D), 1.0, 6.0, ((0, 8), (2, 4))),
        "receptance": bell_draw(seeds[1], (MEMBERS, EPISODE_SYMBOLS, D), 1.0, 6.0, ((0, 8), (2, 4))),
        "keys": bell_draw(seeds[2], (MEMBERS, EPISODE_SYMBOLS, D), 0.05, 0.29882812, ((0, 8), (2, 4))),
        "log_decay": draw_log_decay(jax.random.fold_in(seeds[9], 71), 0),
        "value_weight": bell_draw(seeds[4], (D, D), D ** -0.5, 0.09375, ((0, 8), (1, 4))),
        "noise_in": bell_draw(seeds[5], (MEMBERS, D), 1.0, 6.0, ((0, 8),)),
        "noise_out": bell_draw(seeds[6], (MEMBERS, D), 1.0, 6.0, ((0, 8), (1, 4))),
        "utilities": draw_utilities(jax.random.fold_in(seeds[9], 71), 0),
        "live_length": draw_live_length(jax.random.fold_in(seeds[9], 71), 0),
    }


HIGHEST = lax.Precision.HIGHEST
SIGMA = 0.5

def wkv_block(weighted_key_value_state, recept, masked_keys, masked_decay, value_items):
    cum_log = jnp.cumsum(masked_decay, axis=0)
    span_len = recept.shape[0]
    lower_mask = jnp.arange(span_len)[:, None] >= jnp.arange(span_len)[None, :]
    grown_recept = recept * jnp.exp(cum_log)
    shrunk_keys = masked_keys * jnp.exp(-cum_log)
    scores = jnp.where(lower_mask, jnp.dot(grown_recept, shrunk_keys.T, precision=HIGHEST), 0.0)
    block_out = jnp.dot(grown_recept, weighted_key_value_state, precision=HIGHEST) + jnp.dot(scores, value_items, precision=HIGHEST)
    final_log = cum_log[-1]
    carried = (masked_keys * jnp.exp(final_log[None, :] - cum_log)).T
    weighted_key_value_state = jnp.exp(final_log)[:, None] * weighted_key_value_state + jnp.dot(carried, value_items, precision=HIGHEST)
    return (weighted_key_value_state, block_out)

def wkv_sequence(recept, masked_keys, masked_decay, value_items):
    length, head_size = recept.shape
    block_len = min(32, length)
    weighted_key_value_state = jnp.zeros((head_size, head_size), jnp.float32)
    pieces = []
    for offset in range(0, length, block_len):
        weighted_key_value_state, block_out = wkv_block(weighted_key_value_state, recept[offset:offset + block_len], masked_keys[offset:offset + block_len], masked_decay[offset:offset + block_len], value_items[offset:offset + block_len])
        pieces.append(block_out)
    return jnp.concatenate(pieces, 0)

def to_heads(array_in):
    return array_in.reshape(EPISODE_SYMBOLS, HEADS, HEAD).transpose(1, 0, 2)

def per_member(operands):
    recept, key_rows, decay_rows, value_rows, live_row = operands
    emitted_vector = jax.vmap(wkv_sequence)(to_heads(recept.astype(jnp.float32)), to_heads(key_rows.astype(jnp.float32) * live_row[:, None]), to_heads(decay_rows.astype(jnp.float32) * live_row[:, None]), to_heads(value_rows.astype(jnp.float32)))
    return (emitted_vector.transpose(1, 0, 2).reshape(EPISODE_SYMBOLS, D) * live_row[:, None]).astype(jnp.bfloat16)

def reference(tokens, receptance, keys, log_decay, value_weight, noise_in, noise_out, utilities, live_length):
    live_mask = (jnp.arange(EPISODE_SYMBOLS)[None, :] < live_length[:, None]).astype(jnp.float32)
    base_value = jnp.dot(tokens.reshape(MEMBERS * EPISODE_SYMBOLS, D), value_weight, preferred_element_type=jnp.float32).reshape(MEMBERS, EPISODE_SYMBOLS, D)
    projected = jnp.einsum('mtd,md->mt', tokens.astype(jnp.float32), noise_in.astype(jnp.float32), precision=HIGHEST)
    values = (base_value + SIGMA / math.sqrt(D) * projected[:, :, None] * noise_out.astype(jnp.float32)[:, None, :]).astype(jnp.bfloat16)
    wkv_out = lax.map(per_member, (receptance, keys, log_decay, values, live_mask))
    weighted = noise_in.astype(jnp.float32) * (utilities / math.sqrt(MEMBERS))[:, None]
    update = lax.dot_general(weighted, noise_out.astype(jnp.float32), (((0,), (0,)), ((), ())), precision=HIGHEST)
    return (wkv_out, update)
```

```python
import functools
import math

import jax
import jax.numpy as jnp
from jax import lax
from jax.experimental import pallas as pl
from jax.experimental.pallas import tpu as pltpu
from jax.sharding import PartitionSpec as P

HEAD = 64
SIGMA = 0.5
LANES = 128
WCUTS = 4
TCUTS = 2
MESH = pl.DeviceIdType.MESH
F32 = jnp.float32
BF16 = jnp.bfloat16


def dot_nt(a, b):
    return lax.dot_general(a, b, (((1,), (1,)), ((), ())), preferred_element_type=F32)


def dot_nn(a, b):
    return jnp.dot(a, b, preferred_element_type=F32)


def flip(index, bit):
    return index + bit - 2 * bit * lax.rem(lax.div(index, bit), 2)


def kernel(
    pop,
    tp,
    tok,
    rec,
    key,
    dec,
    w,
    nin,
    nout,
    util,
    live,
    wkv,
    upd,
    tok_buf,
    wbuf,
    s_low,
    s_high,
    proj,
    small_src,
    small_dst,
    upd_buf,
    own_sem,
    upd_sem,
    small_send,
    small_recv,
    group_send,
    group_recv,
    x_send,
    x_recv,
    y_send,
    y_recv,
    c_send,
    c_recv,
    dn_send,
    dn_recv,
    up_send,
    up_recv,
):
    length, width = rec.shape[1], rec.shape[2]
    full = tp * width
    rows = w.shape[0]
    group = pop // 8
    block = rows * group
    cut = block // WCUTS
    tcut = length // TCUTS
    win = upd_buf.shape[0]
    half = length // 2

    p = lax.axis_index("pop")
    k = lax.axis_index("tp")
    q = lax.div(p, group)
    place = lax.rem(p, group)

    def remote(src, dst, send, recv, **where):
        return pltpu.make_async_remote_copy(
            src_ref=src, dst_ref=dst, send_sem=send, recv_sem=recv, device_id=where, device_id_type=MESH
        )

    barrier = pltpu.get_barrier_semaphore()
    for d in range(1, pop):
        pl.semaphore_signal(barrier, inc=1, device_id={"pop": lax.rem(p + d, pop)}, device_id_type=MESH)

    @pl.when(k >= 1)
    def _():
        pl.semaphore_signal(barrier, inc=1, device_id={"tp": k - 1}, device_id_type=MESH)

    @pl.when(k <= tp - 2)
    def _():
        pl.semaphore_signal(barrier, inc=1, device_id={"tp": k + 1}, device_id_type=MESH)

    own_tok = pltpu.make_async_copy(tok.at[0], tok_buf.at[k], own_sem.at[0])
    own_w = pltpu.make_async_copy(w, wbuf.at[pl.ds(pl.multiple_of(p * rows, rows), rows)], own_sem.at[1])
    own_tok.start()
    own_w.start()

    scale = util[0] * (1.0 / math.sqrt(pop))
    weighted = nin[...].astype(F32) * scale
    out_factor = nout[...].astype(F32)
    for dest in range(pop):
        start = dest * rows // LANES * LANES
        small_src[dest, :, 0:win] = weighted[:, start : start + win]
        small_src[dest, :, win : win + width] = out_factor
    neighbours = jnp.where(k >= 1, 1, 0) + jnp.where(k <= tp - 2, 1, 0)
    pl.semaphore_wait(barrier, pop - 1 + neighbours)

    sent = []

    def tok_rows(index, c):
        return tok_buf.at[index, pl.ds(c * tcut, tcut)]

    def down(s, c):
        src = tok.at[0, pl.ds(c * tcut, tcut)] if s == 0 else tok_rows(k + s, c)
        return remote(src, tok_rows(k + s, c), dn_send.at[s, c], dn_recv.at[s, c], tp=k - 1)

    def up(s, c):
        src = tok.at[0, pl.ds(c * tcut, tcut)] if s == 0 else tok_rows(k - s, c)
        return remote(src, tok_rows(k - s, c), up_send.at[s, c], up_recv.at[s, c], tp=k + 1)

    def down_sends(s):
        return (k >= 1) & (k + s <= tp - 1)

    def up_sends(s):
        return (k <= tp - 2) & (k - s >= 0)

    def start_tokens(s, c):
        @pl.when(down_sends(s))
        def _():
            down(s, c).start()

        @pl.when(up_sends(s))
        def _():
            up(s, c).start()

    def take_tokens(s, c):
        @pl.when(k + 1 + s <= tp - 1)
        def _():
            landed = tok_rows(k + 1 + s, c)
            remote(landed, landed, dn_send.at[s, c], dn_recv.at[s, c], tp=k).wait_recv()

        @pl.when(k - 1 - s >= 0)
        def _():
            landed = tok_rows(k - 1 - s, c)
            remote(landed, landed, up_send.at[s, c], up_recv.at[s, c], tp=k).wait_recv()

        if s + 1 <= tp - 2:
            start_tokens(s + 1, c)

    qx, qy, qc = flip(q, 2), flip(q, 4), flip(q, 1)
    qd = flip(qx, 4)

    def piece(index, c):
        return wbuf.at[pl.ds(pl.multiple_of(index * block + c * cut, cut), cut)]

    def own_piece(c):
        return w.at[pl.ds(c * cut, cut)] if group == 1 else piece(q, c)

    def send(src, dst, sems, recvs, slot, target):
        copy = remote(src, dst, sems.at[slot], recvs.at[slot], pop=target * group + place)
        copy.start()
        sent.append(copy)

    def landed(index, c, recvs, slot):
        here = piece(index, c)
        remote(here, here, x_send.at[0], recvs.at[slot], pop=p).wait_recv()

    for c in range(TCUTS):
        start_tokens(0, c)

    if group > 1:
        mine = wbuf.at[pl.ds(pl.multiple_of(p * rows, rows), rows)]
        for d in range(1, group):
            target = q * group + lax.rem(place + d, group)
            copy = remote(w, mine, group_send.at[d - 1], group_recv.at[d - 1], pop=target)
            copy.start()
            sent.append(copy)
        own_w.wait()
        for d in range(1, group):
            origin = q * group + lax.rem(place + group - d, group)
            here = wbuf.at[pl.ds(pl.multiple_of(origin * rows, rows), rows)]
            remote(here, here, group_send.at[d - 1], group_recv.at[d - 1], pop=p).wait_recv()

    x_order = list(range(WCUTS))
    y_order = x_order[WCUTS // 2 :] + x_order[: WCUTS // 2]
    for i in range(WCUTS):
        send(own_piece(x_order[i]), piece(q, x_order[i]), x_send, x_recv, x_order[i], qx)
        send(own_piece(y_order[i]), piece(q, y_order[i]), y_send, y_recv, y_order[i], qy)
        if i == 0:
            for d in range(1, pop):
                target = lax.rem(p + d, pop)
                copy = remote(
                    small_src.at[target], small_dst.at[p], small_send.at[d - 1], small_recv.at[d - 1], pop=target
                )
                copy.start()
                sent.append(copy)
    for i in range(WCUTS):
        send(own_piece(i), piece(q, i), c_send, c_recv, i, qc)
    small_dst[p] = small_src[p]

    def round_of(i):
        if i < WCUTS:
            cx, cy = x_order[i], y_order[i]
            landed(qx, cx, x_recv, cx)
            if i < WCUTS // 2:
                send(piece(qx, cx), piece(qx, cx), y_send, y_recv, WCUTS + i, qy)
            send(piece(qx, cx), piece(qx, cx), c_send, c_recv, WCUTS + cx, qc)
            landed(qy, cy, y_recv, cy)
            if i < WCUTS // 2:
                send(piece(qy, cy), piece(qy, cy), x_send, x_recv, WCUTS + i, qx)
            send(piece(qy, cy), piece(qy, cy), c_send, c_recv, 2 * WCUTS + cy, qc)
        else:
            cx, cy = y_order[i - WCUTS], x_order[i - WCUTS]
            landed(qd, cx, x_recv, i)
            send(piece(qd, cx), piece(qd, cx), c_send, c_recv, 3 * WCUTS + cx, qc)
            landed(qd, cy, y_recv, i)
            send(piece(qd, cy), piece(qd, cy), c_send, c_recv, 3 * WCUTS + cy, qc)

    live_count = live[0]
    lane = lax.broadcasted_iota(jnp.int32, (half, LANES), 1)
    first = (lane < HEAD).astype(F32)
    second = 1.0 - first
    row = lax.broadcasted_iota(jnp.int32, (half, LANES), 0)
    masks = []
    span = 32
    col = lax.broadcasted_iota(jnp.int32, (half, half), 1)
    prow = lax.broadcasted_iota(jnp.int32, (half, half), 0)
    row_block, col_block = lax.div(prow, span), lax.div(col, span)
    diag_mask = (row_block == col_block) & (col <= prow)
    near_mask = (lax.rem(row_block, 2) == 1) & (col_block == row_block - 1)
    far_mask = (row_block >= 2) & (col_block < 2)
    lower = (
        lax.broadcasted_iota(jnp.int32, (length, length), 0) >= lax.broadcasted_iota(jnp.int32, (length, length), 1)
    ).astype(BF16)

    def spread(cum, at, count):
        return jnp.concatenate([jnp.broadcast_to(cum[a : a + 1], (count, LANES)) for a in at], 0)

    def heads_of(queries):
        return jnp.concatenate([queries * first, queries * second], 0).astype(BF16)

    def scores_of(index):
        lanes = pl.ds(pl.multiple_of(index * LANES, LANES), LANES)
        t = lax.broadcasted_iota(jnp.int32, (length, LANES), 0)
        mask = (t < live_count).astype(F32)
        recept = rec[0, :, lanes].astype(F32) * mask
        keys = key[0, :, lanes].astype(F32) * mask
        decay = (dec[0, :, lanes].astype(F32) * mask).astype(BF16)
        cum = dot_nn(lower, decay)
        fade = jnp.exp(-jnp.abs(cum - cum[half - 1 : half]))
        cross = dot_nt(heads_of(recept[half:] * fade[half:]), (keys[:half] * fade[:half]).astype(BF16))
        far = jnp.exp(-jnp.abs(cum - spread(cum, (63, 191), half)))
        near = jnp.exp(-jnp.abs(cum - spread(cum, (31, 95, 159, 223), 64)))
        inner = cum - spread(cum, tuple(range(15, length, span)), span)
        grow, shrink = jnp.exp(inner), jnp.exp(-inner)
        out = []
        for h in range(2):
            part = slice(h * half, (h + 1) * half)
            r, kk = recept[part], keys[part]
            far_s = dot_nt(heads_of(r * far[part]), (kk * far[part]).astype(BF16))
            near_s = dot_nt(heads_of(r * near[part]), (kk * near[part]).astype(BF16))
            diag_s = dot_nt(heads_of(r * grow[part]), (kk * shrink[part]).astype(BF16))
            for a in range(2):
                sel = slice(a * half, (a + 1) * half)
                out.append(
                    jnp.where(
                        diag_mask, diag_s[sel], jnp.where(near_mask, near_s[sel], jnp.where(far_mask, far_s[sel], 0.0))
                    ).astype(BF16)
                )
        cross = cross.astype(BF16)
        s_low[index, :, 0:half] = out[0]
        s_low[index, :, half : 2 * half] = out[1]
        s_high[index, :, 0:half] = cross[:half]
        s_high[index, :, half : 2 * half] = out[2]
        s_high[index, :, 2 * half : 3 * half] = cross[half:]
        s_high[index, :, 3 * half : 4 * half] = out[3]

    pairs = width // LANES
    done = 0

    def score_pairs(begin, end):
        @pl.loop(begin, end)
        def _(index):
            scores_of(index)

    def update_part():
        for d in range(1, pop):
            origin = lax.rem(p + pop - d, pop)
            here = small_dst.at[origin]
            remote(here, here, small_send.at[d - 1], small_recv.at[d - 1], pop=p).wait_recv()
        factor = jnp.concatenate([small_dst[m, :, 0:win] for m in range(pop)], 0)
        high = factor.astype(BF16).astype(F32)
        mid = (factor - high).astype(BF16).astype(F32)
        low = factor - high - mid
        left = jnp.concatenate([high, mid, low], 0).T.astype(BF16)
        for n in range(0, width, 256):
            right = jnp.concatenate([small_dst[m, :, win + n : win + n + 256] for m in range(pop)], 0)
            right = jnp.concatenate([right, right, right], 0).astype(BF16)
            upd_buf[:, n : n + 256] = dot_nn(left, right)

    offset = pl.multiple_of(lax.rem(p * rows, LANES) if rows < LANES else 0, 8)
    upd_copy = pltpu.make_async_copy(upd_buf.at[pl.ds(offset, rows)], upd, upd_sem)

    rounds = WCUTS + WCUTS // 2
    bounds = [pairs * (i + 1) // rounds for i in range(rounds)]
    for i in range(rounds):
        score_pairs(done, bounds[i])
        done = bounds[i]
        round_of(i)
        if i == 1:
            update_part()
            upd_copy.start()
        step, c = divmod(i, TCUTS)
        if step <= tp - 2:
            take_tokens(step, c)

    own_tok.wait()
    for b, index in enumerate((qc, flip(qx, 1), flip(qy, 1), flip(qd, 1))):
        for c in range(WCUTS):
            landed(index, c, c_recv, b * WCUTS + c)
    if group == 1:
        own_w.wait()

    total = jnp.zeros((length, LANES), F32)
    for j in range(tp):
        part = jnp.broadcast_to(nin[:, j * width : (j + 1) * width].astype(F32), (LANES, width)).astype(BF16)
        total = total + dot_nt(tok_buf[j], part)
    proj[...] = total * (SIGMA / math.sqrt(full))

    tile = 2 * LANES

    @pl.loop(0, width // tile)
    def _(n):
        lanes = pl.ds(pl.multiple_of(n * tile, tile), tile)
        base = jnp.concatenate([proj[...], proj[...]], 1) * nout[:, lanes].astype(F32)
        for j in range(tp):
            base = base + dot_nn(tok_buf[j], wbuf[j * width : (j + 1) * width, lanes])
        values = base.astype(BF16)
        for b in range(2):
            pair = values[:, b * LANES : (b + 1) * LANES].astype(F32)
            head_a = jnp.concatenate([pair[:half] * first, pair[half:] * first], 0).astype(BF16)
            head_b = jnp.concatenate([pair[:half] * second, pair[half:] * second], 0).astype(BF16)
            index = n * 2 + b
            low_v = jnp.concatenate([head_a[:half], head_b[:half]], 0)
            high_v = jnp.concatenate([head_a, head_b], 0)
            here = pl.ds(pl.multiple_of(index * LANES, LANES), LANES)
            wkv[0, 0:half, here] = dot_nn(s_low[index], low_v).astype(BF16)
            wkv[0, half:length, here] = dot_nn(s_high[index], high_v).astype(BF16)

    for copy in sent:
        copy.wait_send()
    for s in range(tp - 1):
        for c in range(TCUTS):

            @pl.when(down_sends(s))
            def _():
                down(s, c).wait_send()

            @pl.when(up_sends(s))
            def _():
                up(s, c).wait_send()

    upd_copy.wait()


def body(pop, tp, tokens, receptance, keys, log_decay, value_weight, noise_in, noise_out, utilities, live_length):
    length, width = receptance.shape[1:]
    rows = value_weight.shape[0]
    full = rows * pop
    win = max(rows, LANES)
    pairs = width // LANES
    half = length // 2
    group = pop // 8
    dma = pltpu.SemaphoreType.DMA
    whole = pl.BlockSpec(memory_space=pltpu.VMEM)
    scalar = pl.BlockSpec(memory_space=pltpu.SMEM)
    anywhere = pl.BlockSpec(memory_space=pl.ANY)
    return pl.pallas_call(
        functools.partial(kernel, pop, tp),
        out_shape=(
            jax.ShapeDtypeStruct((1, length, width), BF16),
            jax.ShapeDtypeStruct((rows, width), F32),
        ),
        in_specs=[anywhere, whole, whole, whole, anywhere, whole, whole, scalar, scalar],
        out_specs=(whole, anywhere),
        scratch_shapes=[
            pltpu.VMEM((tp, length, width), BF16),
            pltpu.VMEM((full, width), BF16),
            pltpu.VMEM((pairs, half, 2 * half), BF16),
            pltpu.VMEM((pairs, half, 4 * half), BF16),
            pltpu.VMEM((length, LANES), F32),
            pltpu.VMEM((pop, 1, win + width), F32),
            pltpu.VMEM((pop, 1, win + width), F32),
            pltpu.VMEM((win, width), F32),
            dma((2,)),
            dma,
            dma((pop - 1,)),
            dma((pop - 1,)),
            dma((max(group - 1, 1),)),
            dma((max(group - 1, 1),)),
            dma((2 * WCUTS,)),
            dma((2 * WCUTS,)),
            dma((2 * WCUTS,)),
            dma((2 * WCUTS,)),
            dma((4 * WCUTS,)),
            dma((4 * WCUTS,)),
            dma((tp - 1, TCUTS)),
            dma((tp - 1, TCUTS)),
            dma((tp - 1, TCUTS)),
            dma((tp - 1, TCUTS)),
        ],
        compiler_params=pltpu.CompilerParams(
            collective_id=0, has_side_effects=True, vmem_limit_bytes=48 * 1024 * 1024
        ),
        cost_estimate=pl.CostEstimate(
            flops=2 * length * full * width, bytes_accessed=16 * 1024 * 1024, transcendentals=5 * length * width
        ),
    )(tokens, receptance, keys, log_decay, value_weight, noise_in, noise_out, utilities, live_length)


def solution(mesh):
    return jax.shard_map(
        functools.partial(body, mesh.shape["pop"], mesh.shape["tp"]),
        mesh=mesh,
        in_specs=(
            P("pop", None, "tp"),
            P("pop", None, "tp"),
            P("pop", None, "tp"),
            P("pop", None, "tp"),
            P("pop", "tp"),
            P("pop", None),
            P("pop", "tp"),
            P("pop"),
            P("pop"),
        ),
        out_specs=(P("pop", None, "tp"), P("pop", "tp")),
        check_vma=False,
    )
```

```python
import functools
import math

import jax
import jax.numpy as jnp
from jax import lax
from jax.experimental import pallas as pl
from jax.experimental.pallas import tpu as pltpu
from jax.sharding import PartitionSpec as P

HEAD = 64
SIGMA = 0.5
LANES = 128
WCUTS = 4
TCUTS = 2
MESH = pl.DeviceIdType.MESH
F32 = jnp.float32
BF16 = jnp.bfloat16


def dot_nt(a, b):
    return lax.dot_general(a, b, (((1,), (1,)), ((), ())), preferred_element_type=F32)


def dot_nn(a, b):
    return jnp.dot(a, b, preferred_element_type=F32)


def flip(index, bit):
    return index + bit - 2 * bit * lax.rem(lax.div(index, bit), 2)


def kernel(
    pop,
    tp,
    tok,
    rec_hbm,
    key_hbm,
    dec_hbm,
    w,
    nin_hbm,
    nout_hbm,
    util,
    live,
    wkv,
    upd,
    tok_buf,
    wbuf,
    rec,
    key,
    dec,
    nin,
    nout,
    acc,
    s_low,
    s_high,
    proj,
    small_src,
    small_dst,
    upd_buf,
    own_sem,
    upd_sem,
    small_send,
    small_recv,
    group_send,
    group_recv,
    x_send,
    x_recv,
    y_send,
    y_recv,
    c_send,
    c_recv,
    dn_send,
    dn_recv,
    up_send,
    up_recv,
):
    length, width = rec.shape[1], rec.shape[2]
    full = tp * width
    rows = w.shape[0]
    group = pop // 8
    block = rows * group
    cut = block // WCUTS
    tcut = length // TCUTS
    win = upd_buf.shape[0]
    half = length // 2

    p = lax.axis_index("pop")
    k = lax.axis_index("tp")
    q = lax.div(p, group)
    place = lax.rem(p, group)

    def remote(src, dst, send, recv, **where):
        return pltpu.make_async_remote_copy(
            src_ref=src, dst_ref=dst, send_sem=send, recv_sem=recv, device_id=where, device_id_type=MESH
        )

    barrier = pltpu.get_barrier_semaphore()
    for d in range(1, pop):
        pl.semaphore_signal(barrier, inc=1, device_id={"pop": lax.rem(p + d, pop)}, device_id_type=MESH)

    @pl.when(k >= 1)
    def _():
        pl.semaphore_signal(barrier, inc=1, device_id={"tp": k - 1}, device_id_type=MESH)

    @pl.when(k <= tp - 2)
    def _():
        pl.semaphore_signal(barrier, inc=1, device_id={"tp": k + 1}, device_id_type=MESH)

    own_tok = pltpu.make_async_copy(tok.at[0], tok_buf.at[k], own_sem.at[0])
    own_w = pltpu.make_async_copy(w, wbuf.at[pl.ds(pl.multiple_of(p * rows, rows), rows)], own_sem.at[1])
    loads = [
        pltpu.make_async_copy(src, dst, own_sem.at[2 + i])
        for i, (src, dst) in enumerate(
            ((nin_hbm, nin), (nout_hbm, nout), (dec_hbm, dec), (rec_hbm, rec), (key_hbm, key))
        )
    ]
    for copy in loads:
        copy.start()
    own_tok.start()
    own_w.start()

    neighbours = jnp.where(k >= 1, 1, 0) + jnp.where(k <= tp - 2, 1, 0)
    pl.semaphore_wait(barrier, pop - 1 + neighbours)

    sent = []

    def tok_rows(index, c):
        return tok_buf.at[index, pl.ds(c * tcut, tcut)]

    def down(s, c):
        src = tok.at[0, pl.ds(c * tcut, tcut)] if s == 0 else tok_rows(k + s, c)
        return remote(src, tok_rows(k + s, c), dn_send.at[s, c], dn_recv.at[s, c], tp=k - 1)

    def up(s, c):
        src = tok.at[0, pl.ds(c * tcut, tcut)] if s == 0 else tok_rows(k - s, c)
        return remote(src, tok_rows(k - s, c), up_send.at[s, c], up_recv.at[s, c], tp=k + 1)

    def down_sends(s):
        return (k >= 1) & (k + s <= tp - 1)

    def up_sends(s):
        return (k <= tp - 2) & (k - s >= 0)

    def start_tokens(s, c):
        @pl.when(down_sends(s))
        def _():
            down(s, c).start()

        @pl.when(up_sends(s))
        def _():
            up(s, c).start()

    def take_tokens(s, c):
        @pl.when(k + 1 + s <= tp - 1)
        def _():
            landed = tok_rows(k + 1 + s, c)
            remote(landed, landed, dn_send.at[s, c], dn_recv.at[s, c], tp=k).wait_recv()

        @pl.when(k - 1 - s >= 0)
        def _():
            landed = tok_rows(k - 1 - s, c)
            remote(landed, landed, up_send.at[s, c], up_recv.at[s, c], tp=k).wait_recv()

        if s + 1 <= tp - 2:
            start_tokens(s + 1, c)

    qx, qy, qc = flip(q, 2), flip(q, 4), flip(q, 1)
    qd = flip(qx, 4)

    def piece(index, c):
        return wbuf.at[pl.ds(pl.multiple_of(index * block + c * cut, cut), cut)]

    def own_piece(c):
        return w.at[pl.ds(c * cut, cut)] if group == 1 else piece(q, c)

    def send(src, dst, sems, recvs, slot, target):
        copy = remote(src, dst, sems.at[slot], recvs.at[slot], pop=target * group + place)
        copy.start()
        sent.append(copy)

    def landed(index, c, recvs, slot):
        here = piece(index, c)
        remote(here, here, x_send.at[0], recvs.at[slot], pop=p).wait_recv()

    for c in range(TCUTS):
        start_tokens(0, c)

    if group > 1:
        mine = wbuf.at[pl.ds(pl.multiple_of(p * rows, rows), rows)]
        for d in range(1, group):
            target = q * group + lax.rem(place + d, group)
            copy = remote(w, mine, group_send.at[d - 1], group_recv.at[d - 1], pop=target)
            copy.start()
            sent.append(copy)
        own_w.wait()
        for d in range(1, group):
            origin = q * group + lax.rem(place + group - d, group)
            here = wbuf.at[pl.ds(pl.multiple_of(origin * rows, rows), rows)]
            remote(here, here, group_send.at[d - 1], group_recv.at[d - 1], pop=p).wait_recv()

    x_order = list(range(WCUTS))
    y_order = x_order[WCUTS // 2 :] + x_order[: WCUTS // 2]
    for i in range(WCUTS):
        send(own_piece(x_order[i]), piece(q, x_order[i]), x_send, x_recv, x_order[i], qx)
        send(own_piece(y_order[i]), piece(q, y_order[i]), y_send, y_recv, y_order[i], qy)
    for i in range(WCUTS):
        send(own_piece(i), piece(q, i), c_send, c_recv, i, qc)
    loads[0].wait()
    loads[1].wait()
    scale = util[0] * (1.0 / math.sqrt(pop))
    weighted = nin[...].astype(F32) * scale
    out_factor = nout[...].astype(F32)
    for dest in range(pop):
        start = dest * rows // LANES * LANES
        small_src[dest, :, 0:win] = weighted[:, start : start + win]
        small_src[dest, :, win : win + width] = out_factor
    for d in range(1, pop):
        target = lax.rem(p + d, pop)
        copy = remote(small_src.at[target], small_dst.at[p], small_send.at[d - 1], small_recv.at[d - 1], pop=target)
        copy.start()
        sent.append(copy)
    small_dst[p] = small_src[p]
    for copy in loads[2:]:
        copy.wait()

    def round_of(i):
        if i < WCUTS:
            cx, cy = x_order[i], y_order[i]
            landed(qx, cx, x_recv, cx)
            if i < WCUTS // 2:
                send(piece(qx, cx), piece(qx, cx), y_send, y_recv, WCUTS + i, qy)
            send(piece(qx, cx), piece(qx, cx), c_send, c_recv, WCUTS + cx, qc)
            landed(qy, cy, y_recv, cy)
            if i < WCUTS // 2:
                send(piece(qy, cy), piece(qy, cy), x_send, x_recv, WCUTS + i, qx)
            send(piece(qy, cy), piece(qy, cy), c_send, c_recv, 2 * WCUTS + cy, qc)
        else:
            cx, cy = y_order[i - WCUTS], x_order[i - WCUTS]
            landed(qd, cx, x_recv, i)
            send(piece(qd, cx), piece(qd, cx), c_send, c_recv, 3 * WCUTS + cx, qc)
            landed(qd, cy, y_recv, i)
            send(piece(qd, cy), piece(qd, cy), c_send, c_recv, 3 * WCUTS + cy, qc)

    live_count = live[0]
    lane = lax.broadcasted_iota(jnp.int32, (half, LANES), 1)
    first = (lane < HEAD).astype(F32)
    second = 1.0 - first
    row = lax.broadcasted_iota(jnp.int32, (half, LANES), 0)
    masks = []
    span = 32
    col = lax.broadcasted_iota(jnp.int32, (half, half), 1)
    prow = lax.broadcasted_iota(jnp.int32, (half, half), 0)
    row_block, col_block = lax.div(prow, span), lax.div(col, span)
    diag_mask = (row_block == col_block) & (col <= prow)
    near_mask = (lax.rem(row_block, 2) == 1) & (col_block == row_block - 1)
    far_mask = (row_block >= 2) & (col_block < 2)
    lower = (
        lax.broadcasted_iota(jnp.int32, (length, length), 0) >= lax.broadcasted_iota(jnp.int32, (length, length), 1)
    ).astype(BF16)

    def spread(cum, at, count):
        return jnp.concatenate([jnp.broadcast_to(cum[a : a + 1], (count, LANES)) for a in at], 0)

    def heads_of(queries):
        high = queries.astype(BF16).astype(F32)
        low = queries - high
        terms = [jnp.concatenate([high * m, low * m], 1) for m in (first, second)]
        return jnp.concatenate(terms, 0).astype(BF16)

    def twice(keys):
        keys = keys.astype(BF16)
        return jnp.concatenate([keys, keys], 1)

    def scores_of(index):
        lanes = pl.ds(pl.multiple_of(index * LANES, LANES), LANES)
        t = lax.broadcasted_iota(jnp.int32, (length, LANES), 0)
        mask = (t < live_count).astype(F32)
        recept = rec[0, :, lanes].astype(F32) * mask
        keys = key[0, :, lanes].astype(F32) * mask
        decay = (dec[0, :, lanes].astype(F32) * mask).astype(BF16)
        cum = dot_nn(lower, decay)
        fade = jnp.exp(-jnp.abs(cum - cum[half - 1 : half]))
        cross = dot_nt(heads_of(recept[half:] * fade[half:]), twice(keys[:half] * fade[:half]))
        far = jnp.exp(-jnp.abs(cum - spread(cum, (63, 191), half)))
        near = jnp.exp(-jnp.abs(cum - spread(cum, (31, 95, 159, 223), 64)))
        inner = cum - spread(cum, tuple(range(15, length, span)), span)
        grow, shrink = jnp.exp(inner), jnp.exp(-inner)
        out = []
        for h in range(2):
            part = slice(h * half, (h + 1) * half)
            r, kk = recept[part], keys[part]
            far_s = dot_nt(heads_of(r * far[part]), twice(kk * far[part]))
            near_s = dot_nt(heads_of(r * near[part]), twice(kk * near[part]))
            diag_s = dot_nt(heads_of(r * grow[part]), twice(kk * shrink[part]))
            for a in range(2):
                sel = slice(a * half, (a + 1) * half)
                out.append(
                    jnp.where(
                        diag_mask, diag_s[sel], jnp.where(near_mask, near_s[sel], jnp.where(far_mask, far_s[sel], 0.0))
                    ).astype(BF16)
                )
        cross = cross.astype(BF16)
        s_low[index, :, 0:half] = out[0]
        s_low[index, :, half : 2 * half] = out[1]
        s_high[index, :, 0:half] = cross[:half]
        s_high[index, :, half : 2 * half] = out[2]
        s_high[index, :, 2 * half : 3 * half] = cross[half:]
        s_high[index, :, 3 * half : 4 * half] = out[3]

    pairs = width // LANES
    done = 0

    def score_pairs(begin, end):
        @pl.loop(begin, end)
        def _(index):
            scores_of(index)

    def update_part():
        for d in range(1, pop):
            origin = lax.rem(p + pop - d, pop)
            here = small_dst.at[origin]
            remote(here, here, small_send.at[d - 1], small_recv.at[d - 1], pop=p).wait_recv()
        factor = jnp.concatenate([small_dst[m, :, 0:win] for m in range(pop)], 0)
        high = factor.astype(BF16).astype(F32)
        mid = (factor - high).astype(BF16).astype(F32)
        low = factor - high - mid
        left = jnp.concatenate([high, mid, low], 0).T.astype(BF16)
        for n in range(0, width, 256):
            right = jnp.concatenate([small_dst[m, :, win + n : win + n + 256] for m in range(pop)], 0)
            right = jnp.concatenate([right, right, right], 0).astype(BF16)
            upd_buf[:, n : n + 256] = dot_nn(left, right)

    offset = pl.multiple_of(lax.rem(p * rows, LANES) if rows < LANES else 0, 8)
    upd_copy = pltpu.make_async_copy(upd_buf.at[pl.ds(offset, rows)], upd, upd_sem)

    tile = 2 * LANES
    qxc, qyc, qdc = flip(qx, 1), flip(qy, 1), flip(qd, 1)
    near_blocks = (q, qc, qx, qxc, qy, qyc)
    last_blocks = (qd, qdc)
    all_pieces = tuple(range(WCUTS))

    def distance(index):
        j = lax.div(index * block, width)
        return jnp.maximum(j - k, k - j)

    def is_far(index):
        return distance(index) >= tp - 1

    def multiply(index, pieces, begin, end):
        j = lax.div(index * block, width)
        base = lax.rem(index * block, width)
        if pieces == all_pieces:
            spans = [(0, block)]
        else:
            spans = [(c * cut, cut) for c in pieces]

        @pl.loop(0, width // tile)
        def _(n):
            lanes = pl.ds(pl.multiple_of(n * tile, tile), tile)
            left = [tok_buf[j, begin:end, pl.ds(pl.multiple_of(base + o, LANES), size)] for o, size in spans]
            right = [wbuf[pl.ds(pl.multiple_of(index * block + o, LANES), size), lanes] for o, size in spans]
            if len(spans) > 1:
                left, right = [jnp.concatenate(left, 1)], [jnp.concatenate(right, 0)]
            acc[begin:end, lanes] += dot_nn(left[0], right[0])

    def project(j):
        part = jnp.broadcast_to(nin[:, j * width : (j + 1) * width].astype(F32), (LANES, width)).astype(BF16)
        proj[...] += dot_nt(tok_buf[j], part)

    def arrived(index, b, pieces):
        for c in pieces:
            landed(index, c, c_recv, b * WCUTS + c)

    acc[...] = jnp.zeros_like(acc)
    proj[...] = jnp.zeros_like(proj)
    rounds = WCUTS + WCUTS // 2
    bounds = [pairs * share // 8 for share in (3, 5, 7, 8, 8, 8)]
    early = (x_order[0], y_order[0])
    late = (x_order[1], y_order[1])
    for i in range(rounds):
        score_pairs(done, bounds[i])
        done = bounds[i]
        round_of(i)
        step, c = divmod(i, TCUTS)
        if step <= tp - 2:
            take_tokens(step, c)
        if i == 2:
            update_part()
            upd_copy.start()
        if i == 3:
            own_tok.wait()
            if group == 1:
                own_w.wait()
            for b, index in enumerate((qc, qxc, qyc)):
                arrived(index, b, all_pieces)
            for index in near_blocks:

                @pl.when(jnp.logical_not(is_far(index)))
                def _():
                    multiply(index, all_pieces, 0, length)

            for j in range(tp):

                @pl.when(jnp.maximum(j - k, k - j) < tp - 1)
                def _():
                    project(j)

        if i == 4:
            arrived(qdc, 3, early)
            for index in near_blocks:

                @pl.when(is_far(index))
                def _():
                    multiply(index, all_pieces, 0, half)

            for index in last_blocks:

                @pl.when(is_far(index))
                def _():
                    multiply(index, early, 0, half)

                @pl.when(jnp.logical_not(is_far(index)))
                def _():
                    multiply(index, early, 0, length)

    for index in near_blocks:

        @pl.when(is_far(index))
        def _():
            multiply(index, all_pieces, half, length)

    for j in range(tp):

        @pl.when(jnp.maximum(j - k, k - j) >= tp - 1)
        def _():
            project(j)

    arrived(qdc, 3, late)
    for index in last_blocks:

        @pl.when(is_far(index))
        def _():
            multiply(index, late, 0, half)
            multiply(index, all_pieces, half, length)

        @pl.when(jnp.logical_not(is_far(index)))
        def _():
            multiply(index, late, 0, length)

    factor = proj[...] * (SIGMA / math.sqrt(full))

    @pl.loop(0, width // tile)
    def _(n):
        lanes = pl.ds(pl.multiple_of(n * tile, tile), tile)
        base = acc[:, lanes] + jnp.concatenate([factor, factor], 1) * nout[:, lanes].astype(F32)
        values = base.astype(BF16)
        for b in range(2):
            pair = values[:, b * LANES : (b + 1) * LANES].astype(F32)
            head_a = jnp.concatenate([pair[:half] * first, pair[half:] * first], 0).astype(BF16)
            head_b = jnp.concatenate([pair[:half] * second, pair[half:] * second], 0).astype(BF16)
            index = n * 2 + b
            low_v = jnp.concatenate([head_a[:half], head_b[:half]], 0)
            high_v = jnp.concatenate([head_a, head_b], 0)
            here = pl.ds(pl.multiple_of(index * LANES, LANES), LANES)
            wkv[0, 0:half, here] = dot_nn(s_low[index], low_v).astype(BF16)
            wkv[0, half:length, here] = dot_nn(s_high[index], high_v).astype(BF16)

    for copy in sent:
        copy.wait_send()
    for s in range(tp - 1):
        for c in range(TCUTS):

            @pl.when(down_sends(s))
            def _():
                down(s, c).wait_send()

            @pl.when(up_sends(s))
            def _():
                up(s, c).wait_send()

    upd_copy.wait()


def body(pop, tp, tokens, receptance, keys, log_decay, value_weight, noise_in, noise_out, utilities, live_length):
    length, width = receptance.shape[1:]
    rows = value_weight.shape[0]
    full = rows * pop
    win = max(rows, LANES)
    pairs = width // LANES
    half = length // 2
    group = pop // 8
    dma = pltpu.SemaphoreType.DMA
    whole = pl.BlockSpec(memory_space=pltpu.VMEM)
    scalar = pl.BlockSpec(memory_space=pltpu.SMEM)
    anywhere = pl.BlockSpec(memory_space=pl.ANY)
    hbm = pl.BlockSpec(memory_space=pltpu.HBM)
    return pl.pallas_call(
        functools.partial(kernel, pop, tp),
        out_shape=(
            jax.ShapeDtypeStruct((1, length, width), BF16),
            jax.ShapeDtypeStruct((rows, width), F32),
        ),
        in_specs=[hbm] * 7 + [scalar] * 2,
        out_specs=(whole, anywhere),
        scratch_shapes=[
            pltpu.VMEM((tp, length, width), BF16),
            pltpu.VMEM((full, width), BF16),
            pltpu.VMEM((1, length, width), BF16),
            pltpu.VMEM((1, length, width), BF16),
            pltpu.VMEM((1, length, width), BF16),
            pltpu.VMEM((1, full), BF16),
            pltpu.VMEM((1, width), BF16),
            pltpu.VMEM((length, width), F32),
            pltpu.VMEM((pairs, half, 2 * half), BF16),
            pltpu.VMEM((pairs, half, 4 * half), BF16),
            pltpu.VMEM((length, LANES), F32),
            pltpu.VMEM((pop, 1, win + width), F32),
            pltpu.VMEM((pop, 1, win + width), F32),
            pltpu.VMEM((win, width), F32),
            dma((7,)),
            dma,
            dma((pop - 1,)),
            dma((pop - 1,)),
            dma((max(group - 1, 1),)),
            dma((max(group - 1, 1),)),
            dma((2 * WCUTS,)),
            dma((2 * WCUTS,)),
            dma((2 * WCUTS,)),
            dma((2 * WCUTS,)),
            dma((4 * WCUTS,)),
            dma((4 * WCUTS,)),
            dma((tp - 1, TCUTS)),
            dma((tp - 1, TCUTS)),
            dma((tp - 1, TCUTS)),
            dma((tp - 1, TCUTS)),
        ],
        compiler_params=pltpu.CompilerParams(
            collective_id=0, has_side_effects=True, vmem_limit_bytes=48 * 1024 * 1024
        ),
        cost_estimate=pl.CostEstimate(
            flops=2 * length * full * width, bytes_accessed=16 * 1024 * 1024, transcendentals=5 * length * width
        ),
    )(tokens, receptance, keys, log_decay, value_weight, noise_in, noise_out, utilities, live_length)


def solution(mesh):
    return jax.shard_map(
        functools.partial(body, mesh.shape["pop"], mesh.shape["tp"]),
        mesh=mesh,
        in_specs=(
            P("pop", None, "tp"),
            P("pop", None, "tp"),
            P("pop", None, "tp"),
            P("pop", None, "tp"),
            P("pop", "tp"),
            P("pop", None),
            P("pop", "tp"),
            P("pop"),
            P("pop"),
        ),
        out_specs=(P("pop", None, "tp"), P("pop", "tp")),
        check_vma=False,
    )
```

```python
import functools
import math

import jax
import jax.numpy as jnp
from jax import lax
from jax.experimental import pallas as pl
from jax.experimental.pallas import tpu as pltpu
from jax.sharding import PartitionSpec as P

HEAD = 64
SIGMA = 0.5
LANES = 128
WCUTS = 4
TCUTS = 2
MESH = pl.DeviceIdType.MESH
F32 = jnp.float32
BF16 = jnp.bfloat16


def dot_nt(a, b):
    return lax.dot_general(a, b, (((1,), (1,)), ((), ())), preferred_element_type=F32)


def dot_nn(a, b):
    return jnp.dot(a, b, preferred_element_type=F32)


def flip(index, bit):
    return index + bit - 2 * bit * lax.rem(lax.div(index, bit), 2)


def kernel(
    pop,
    tp,
    tok,
    rec_hbm,
    key_hbm,
    dec_hbm,
    w,
    nin_hbm,
    nout_hbm,
    util,
    live,
    wkv,
    upd,
    tok_buf,
    wbuf,
    rec,
    key,
    dec,
    nin,
    nout,
    acc,
    s_low,
    s_high,
    proj,
    small_src,
    small_dst,
    upd_buf,
    own_sem,
    upd_sem,
    small_send,
    small_recv,
    group_send,
    group_recv,
    x_send,
    x_recv,
    y_send,
    y_recv,
    c_send,
    c_recv,
    dn_send,
    dn_recv,
    up_send,
    up_recv,
):
    length, width = rec.shape[1], rec.shape[2]
    full = tp * width
    rows = w.shape[0]
    group = pop // 8
    block = rows * group
    cut = block // WCUTS
    tcut = length // TCUTS
    win = upd_buf.shape[0]
    half = length // 2

    p = lax.axis_index("pop")
    k = lax.axis_index("tp")
    q = lax.div(p, group)
    place = lax.rem(p, group)

    def remote(src, dst, send, recv, **where):
        return pltpu.make_async_remote_copy(
            src_ref=src, dst_ref=dst, send_sem=send, recv_sem=recv, device_id=where, device_id_type=MESH
        )

    barrier = pltpu.get_barrier_semaphore()
    for d in range(1, pop):
        pl.semaphore_signal(barrier, inc=1, device_id={"pop": lax.rem(p + d, pop)}, device_id_type=MESH)

    @pl.when(k >= 1)
    def _():
        pl.semaphore_signal(barrier, inc=1, device_id={"tp": k - 1}, device_id_type=MESH)

    @pl.when(k <= tp - 2)
    def _():
        pl.semaphore_signal(barrier, inc=1, device_id={"tp": k + 1}, device_id_type=MESH)

    own_tok = pltpu.make_async_copy(tok.at[0], tok_buf.at[k], own_sem.at[0])
    own_w = pltpu.make_async_copy(w, wbuf.at[pl.ds(pl.multiple_of(p * rows, rows), rows)], own_sem.at[1])
    loads = [
        pltpu.make_async_copy(src, dst, own_sem.at[2 + i])
        for i, (src, dst) in enumerate(
            ((nin_hbm, nin), (nout_hbm, nout), (dec_hbm, dec), (rec_hbm, rec), (key_hbm, key))
        )
    ]
    for copy in loads:
        copy.start()
    own_tok.start()
    own_w.start()

    neighbours = jnp.where(k >= 1, 1, 0) + jnp.where(k <= tp - 2, 1, 0)
    pl.semaphore_wait(barrier, pop - 1 + neighbours)

    sent = []

    def tok_rows(index, c):
        return tok_buf.at[index, pl.ds(c * tcut, tcut)]

    def down(s, c):
        src = tok.at[0, pl.ds(c * tcut, tcut)] if s == 0 else tok_rows(k + s, c)
        return remote(src, tok_rows(k + s, c), dn_send.at[s, c], dn_recv.at[s, c], tp=k - 1)

    def up(s, c):
        src = tok.at[0, pl.ds(c * tcut, tcut)] if s == 0 else tok_rows(k - s, c)
        return remote(src, tok_rows(k - s, c), up_send.at[s, c], up_recv.at[s, c], tp=k + 1)

    def down_sends(s):
        return (k >= 1) & (k + s <= tp - 1)

    def up_sends(s):
        return (k <= tp - 2) & (k - s >= 0)

    def start_tokens(s, c):
        @pl.when(down_sends(s))
        def _():
            down(s, c).start()

        @pl.when(up_sends(s))
        def _():
            up(s, c).start()

    def take_tokens(s, c):
        @pl.when(k + 1 + s <= tp - 1)
        def _():
            landed = tok_rows(k + 1 + s, c)
            remote(landed, landed, dn_send.at[s, c], dn_recv.at[s, c], tp=k).wait_recv()

        @pl.when(k - 1 - s >= 0)
        def _():
            landed = tok_rows(k - 1 - s, c)
            remote(landed, landed, up_send.at[s, c], up_recv.at[s, c], tp=k).wait_recv()

        if s + 1 <= tp - 2:
            start_tokens(s + 1, c)

    qx, qy, qc = flip(q, 2), flip(q, 4), flip(q, 1)
    qd = flip(qx, 4)

    def piece(index, c):
        return wbuf.at[pl.ds(pl.multiple_of(index * block + c * cut, cut), cut)]

    def own_piece(c):
        return w.at[pl.ds(c * cut, cut)] if group == 1 else piece(q, c)

    def send(src, dst, sems, recvs, slot, target):
        copy = remote(src, dst, sems.at[slot], recvs.at[slot], pop=target * group + place)
        copy.start()
        sent.append(copy)

    def landed(index, c, recvs, slot):
        here = piece(index, c)
        remote(here, here, x_send.at[0], recvs.at[slot], pop=p).wait_recv()

    for c in range(TCUTS):
        start_tokens(0, c)

    if group > 1:
        mine = wbuf.at[pl.ds(pl.multiple_of(p * rows, rows), rows)]
        for d in range(1, group):
            target = q * group + lax.rem(place + d, group)
            copy = remote(w, mine, group_send.at[d - 1], group_recv.at[d - 1], pop=target)
            copy.start()
            sent.append(copy)
        own_w.wait()
        for d in range(1, group):
            origin = q * group + lax.rem(place + group - d, group)
            here = wbuf.at[pl.ds(pl.multiple_of(origin * rows, rows), rows)]
            remote(here, here, group_send.at[d - 1], group_recv.at[d - 1], pop=p).wait_recv()

    x_order = list(range(WCUTS))
    y_order = x_order[WCUTS // 2 :] + x_order[: WCUTS // 2]
    for i in range(WCUTS):
        send(own_piece(x_order[i]), piece(q, x_order[i]), x_send, x_recv, x_order[i], qx)
        send(own_piece(y_order[i]), piece(q, y_order[i]), y_send, y_recv, y_order[i], qy)
    for i in range(WCUTS):
        send(own_piece(i), piece(q, i), c_send, c_recv, i, qc)
    loads[0].wait()
    loads[1].wait()
    scale = util[0] * (1.0 / math.sqrt(pop))
    weighted = nin[...].astype(F32) * scale
    out_factor = nout[...].astype(F32)
    for dest in range(pop):
        start = dest * rows // LANES * LANES
        small_src[dest, :, 0:win] = weighted[:, start : start + win]
        small_src[dest, :, win : win + width] = out_factor
    for d in range(1, pop):
        target = lax.rem(p + d, pop)
        copy = remote(small_src.at[target], small_dst.at[p], small_send.at[d - 1], small_recv.at[d - 1], pop=target)
        copy.start()
        sent.append(copy)
    small_dst[p] = small_src[p]
    for copy in loads[2:]:
        copy.wait()

    def round_of(i):
        if i < WCUTS:
            cx, cy = x_order[i], y_order[i]
            landed(qx, cx, x_recv, cx)
            if i < WCUTS // 2:
                send(piece(qx, cx), piece(qx, cx), y_send, y_recv, WCUTS + i, qy)
            send(piece(qx, cx), piece(qx, cx), c_send, c_recv, WCUTS + cx, qc)
            landed(qy, cy, y_recv, cy)
            if i < WCUTS // 2:
                send(piece(qy, cy), piece(qy, cy), x_send, x_recv, WCUTS + i, qx)
            send(piece(qy, cy), piece(qy, cy), c_send, c_recv, 2 * WCUTS + cy, qc)
        else:
            cx, cy = y_order[i - WCUTS], x_order[i - WCUTS]
            landed(qd, cx, x_recv, i)
            send(piece(qd, cx), piece(qd, cx), c_send, c_recv, 3 * WCUTS + cx, qc)
            landed(qd, cy, y_recv, i)
            send(piece(qd, cy), piece(qd, cy), c_send, c_recv, 3 * WCUTS + cy, qc)

    live_count = live[0]
    lane = lax.broadcasted_iota(jnp.int32, (half, LANES), 1)
    first = (lane < HEAD).astype(F32)
    second = 1.0 - first
    row = lax.broadcasted_iota(jnp.int32, (half, LANES), 0)
    masks = []
    span = 32
    col = lax.broadcasted_iota(jnp.int32, (half, half), 1)
    prow = lax.broadcasted_iota(jnp.int32, (half, half), 0)
    row_block, col_block = lax.div(prow, span), lax.div(col, span)
    diag_mask = (row_block == col_block) & (col <= prow)
    near_mask = (lax.rem(row_block, 2) == 1) & (col_block == row_block - 1)
    far_mask = (row_block >= 2) & (col_block < 2)
    lower = (
        lax.broadcasted_iota(jnp.int32, (length, length), 0) >= lax.broadcasted_iota(jnp.int32, (length, length), 1)
    ).astype(BF16)

    def spread(cum, at, count):
        return jnp.concatenate([jnp.broadcast_to(cum[a : a + 1], (count, LANES)) for a in at], 0)

    def heads_of(queries):
        return jnp.concatenate([queries * first, queries * second], 0).astype(BF16)

    def scores_of(index):
        lanes = pl.ds(pl.multiple_of(index * LANES, LANES), LANES)
        t = lax.broadcasted_iota(jnp.int32, (length, LANES), 0)
        mask = (t < live_count).astype(F32)
        recept = rec[0, :, lanes].astype(F32) * mask
        keys = key[0, :, lanes].astype(F32) * mask
        decay = (dec[0, :, lanes].astype(F32) * mask).astype(BF16)
        cum = dot_nn(lower, decay)
        fade = jnp.exp(-jnp.abs(cum - cum[half - 1 : half]))
        cross = dot_nt(heads_of(recept[half:] * fade[half:]), (keys[:half] * fade[:half]).astype(BF16))
        far = jnp.exp(-jnp.abs(cum - spread(cum, (63, 191), half)))
        near = jnp.exp(-jnp.abs(cum - spread(cum, (31, 95, 159, 223), 64)))
        inner = cum - spread(cum, tuple(range(15, length, span)), span)
        grow, shrink = jnp.exp(inner), jnp.exp(-inner)
        out = []
        for h in range(2):
            part = slice(h * half, (h + 1) * half)
            r, kk = recept[part], keys[part]
            far_s = dot_nt(heads_of(r * far[part]), (kk * far[part]).astype(BF16))
            near_s = dot_nt(heads_of(r * near[part]), (kk * near[part]).astype(BF16))
            diag_s = dot_nt(heads_of(r * grow[part]), (kk * shrink[part]).astype(BF16))
            for a in range(2):
                sel = slice(a * half, (a + 1) * half)
                out.append(
                    jnp.where(
                        diag_mask, diag_s[sel], jnp.where(near_mask, near_s[sel], jnp.where(far_mask, far_s[sel], 0.0))
                    ).astype(BF16)
                )
        cross = cross.astype(BF16)
        s_low[index, :, 0:half] = out[0]
        s_low[index, :, half : 2 * half] = out[1]
        s_high[index, :, 0:half] = cross[:half]
        s_high[index, :, half : 2 * half] = out[2]
        s_high[index, :, 2 * half : 3 * half] = cross[half:]
        s_high[index, :, 3 * half : 4 * half] = out[3]

    pairs = width // LANES
    done = 0

    def score_pairs(begin, end):
        @pl.loop(begin // 2, end // 2)
        def _(index):
            scores_of(index * 2)
            scores_of(index * 2 + 1)

    def update_part():
        for d in range(1, pop):
            origin = lax.rem(p + pop - d, pop)
            here = small_dst.at[origin]
            remote(here, here, small_send.at[d - 1], small_recv.at[d - 1], pop=p).wait_recv()
        factor = jnp.concatenate([small_dst[m, :, 0:win] for m in range(pop)], 0)
        high = factor.astype(BF16).astype(F32)
        mid = (factor - high).astype(BF16).astype(F32)
        low = factor - high - mid
        left = jnp.concatenate([high, mid, low], 0).T.astype(BF16)
        for n in range(0, width, 256):
            right = jnp.concatenate([small_dst[m, :, win + n : win + n + 256] for m in range(pop)], 0)
            right = jnp.concatenate([right, right, right], 0).astype(BF16)
            upd_buf[:, n : n + 256] = dot_nn(left, right)

    offset = pl.multiple_of(lax.rem(p * rows, LANES) if rows < LANES else 0, 8)
    upd_copy = pltpu.make_async_copy(upd_buf.at[pl.ds(offset, rows)], upd, upd_sem)

    tile = 2 * LANES
    qxc, qyc, qdc = flip(qx, 1), flip(qy, 1), flip(qd, 1)
    near_blocks = (q, qc, qx, qxc, qy, qyc)
    last_blocks = (qd, qdc)
    all_pieces = tuple(range(WCUTS))

    def distance(index):
        j = lax.div(index * block, width)
        return jnp.maximum(j - k, k - j)

    def is_far(index):
        return distance(index) >= tp - 1

    def multiply(index, pieces, begin, end):
        j = lax.div(index * block, width)
        base = lax.rem(index * block, width)
        if pieces == all_pieces:
            spans = [(0, block)]
        else:
            spans = [(c * cut, cut) for c in pieces]

        @pl.loop(0, width // tile)
        def _(n):
            lanes = pl.ds(pl.multiple_of(n * tile, tile), tile)
            left = [tok_buf[j, begin:end, pl.ds(pl.multiple_of(base + o, LANES), size)] for o, size in spans]
            right = [wbuf[pl.ds(pl.multiple_of(index * block + o, LANES), size), lanes] for o, size in spans]
            if len(spans) > 1:
                left, right = [jnp.concatenate(left, 1)], [jnp.concatenate(right, 0)]
            acc[begin:end, lanes] += dot_nn(left[0], right[0])

    def project(j):
        part = jnp.broadcast_to(nin[:, j * width : (j + 1) * width].astype(F32), (LANES, width)).astype(BF16)
        proj[...] += dot_nt(tok_buf[j], part)

    def arrived(index, b, pieces):
        for c in pieces:
            landed(index, c, c_recv, b * WCUTS + c)

    acc[...] = jnp.zeros_like(acc)
    proj[...] = jnp.zeros_like(proj)
    rounds = WCUTS + WCUTS // 2
    bounds = [pairs * share // 8 for share in (2, 4, 6, 6, 8, 8)]
    early = (x_order[0], y_order[0])
    late = (x_order[1], y_order[1])
    for i in range(rounds):
        score_pairs(done, bounds[i])
        done = bounds[i]
        round_of(i)
        step, c = divmod(i, TCUTS)
        if step <= tp - 2:
            take_tokens(step, c)
        if i == 3:
            update_part()
            upd_copy.start()
            own_tok.wait()
            if group == 1:
                own_w.wait()
            for b, index in enumerate((qc, qxc, qyc)):
                arrived(index, b, all_pieces)
            for index in near_blocks:

                @pl.when(jnp.logical_not(is_far(index)))
                def _():
                    multiply(index, all_pieces, 0, length)

            for j in range(tp):

                @pl.when(jnp.maximum(j - k, k - j) < tp - 1)
                def _():
                    project(j)

        if i == 4:
            arrived(qdc, 3, early)
            for index in near_blocks:

                @pl.when(is_far(index))
                def _():
                    multiply(index, all_pieces, 0, half)

            for index in last_blocks:

                @pl.when(is_far(index))
                def _():
                    multiply(index, early, 0, half)

                @pl.when(jnp.logical_not(is_far(index)))
                def _():
                    multiply(index, early, 0, length)

    for index in near_blocks:

        @pl.when(is_far(index))
        def _():
            multiply(index, all_pieces, half, length)

    for j in range(tp):

        @pl.when(jnp.maximum(j - k, k - j) >= tp - 1)
        def _():
            project(j)

    arrived(qdc, 3, late)
    for index in last_blocks:

        @pl.when(is_far(index))
        def _():
            multiply(index, late, 0, half)
            multiply(index, all_pieces, half, length)

        @pl.when(jnp.logical_not(is_far(index)))
        def _():
            multiply(index, late, 0, length)

    factor = proj[...] * (SIGMA / math.sqrt(full))

    @pl.loop(0, width // tile)
    def _(n):
        lanes = pl.ds(pl.multiple_of(n * tile, tile), tile)
        base = acc[:, lanes] + jnp.concatenate([factor, factor], 1) * nout[:, lanes].astype(F32)
        values = base.astype(BF16)
        for b in range(2):
            pair = values[:, b * LANES : (b + 1) * LANES].astype(F32)
            head_a = jnp.concatenate([pair[:half] * first, pair[half:] * first], 0).astype(BF16)
            head_b = jnp.concatenate([pair[:half] * second, pair[half:] * second], 0).astype(BF16)
            index = n * 2 + b
            low_v = jnp.concatenate([head_a[:half], head_b[:half]], 0)
            high_v = jnp.concatenate([head_a, head_b], 0)
            here = pl.ds(pl.multiple_of(index * LANES, LANES), LANES)
            wkv[0, 0:half, here] = dot_nn(s_low[index], low_v).astype(BF16)
            wkv[0, half:length, here] = dot_nn(s_high[index], high_v).astype(BF16)

    for copy in sent:
        copy.wait_send()
    for s in range(tp - 1):
        for c in range(TCUTS):

            @pl.when(down_sends(s))
            def _():
                down(s, c).wait_send()

            @pl.when(up_sends(s))
            def _():
                up(s, c).wait_send()

    upd_copy.wait()


def body(pop, tp, tokens, receptance, keys, log_decay, value_weight, noise_in, noise_out, utilities, live_length):
    length, width = receptance.shape[1:]
    rows = value_weight.shape[0]
    full = rows * pop
    win = max(rows, LANES)
    pairs = width // LANES
    half = length // 2
    group = pop // 8
    dma = pltpu.SemaphoreType.DMA
    whole = pl.BlockSpec(memory_space=pltpu.VMEM)
    scalar = pl.BlockSpec(memory_space=pltpu.SMEM)
    anywhere = pl.BlockSpec(memory_space=pl.ANY)
    hbm = pl.BlockSpec(memory_space=pltpu.HBM)
    return pl.pallas_call(
        functools.partial(kernel, pop, tp),
        out_shape=(
            jax.ShapeDtypeStruct((1, length, width), BF16),
            jax.ShapeDtypeStruct((rows, width), F32),
        ),
        in_specs=[hbm] * 7 + [scalar] * 2,
        out_specs=(whole, anywhere),
        scratch_shapes=[
            pltpu.VMEM((tp, length, width), BF16),
            pltpu.VMEM((full, width), BF16),
            pltpu.VMEM((1, length, width), BF16),
            pltpu.VMEM((1, length, width), BF16),
            pltpu.VMEM((1, length, width), BF16),
            pltpu.VMEM((1, full), BF16),
            pltpu.VMEM((1, width), BF16),
            pltpu.VMEM((length, width), F32),
            pltpu.VMEM((pairs, half, 2 * half), BF16),
            pltpu.VMEM((pairs, half, 4 * half), BF16),
            pltpu.VMEM((length, LANES), F32),
            pltpu.VMEM((pop, 1, win + width), F32),
            pltpu.VMEM((pop, 1, win + width), F32),
            pltpu.VMEM((win, width), F32),
            dma((7,)),
            dma,
            dma((pop - 1,)),
            dma((pop - 1,)),
            dma((max(group - 1, 1),)),
            dma((max(group - 1, 1),)),
            dma((2 * WCUTS,)),
            dma((2 * WCUTS,)),
            dma((2 * WCUTS,)),
            dma((2 * WCUTS,)),
            dma((4 * WCUTS,)),
            dma((4 * WCUTS,)),
            dma((tp - 1, TCUTS)),
            dma((tp - 1, TCUTS)),
            dma((tp - 1, TCUTS)),
            dma((tp - 1, TCUTS)),
        ],
        compiler_params=pltpu.CompilerParams(
            collective_id=0, has_side_effects=True, vmem_limit_bytes=63 * 1024 * 1024
        ),
        cost_estimate=pl.CostEstimate(
            flops=2 * length * full * width, bytes_accessed=16 * 1024 * 1024, transcendentals=5 * length * width
        ),
    )(tokens, receptance, keys, log_decay, value_weight, noise_in, noise_out, utilities, live_length)


def solution(mesh):
    return jax.shard_map(
        functools.partial(body, mesh.shape["pop"], mesh.shape["tp"]),
        mesh=mesh,
        in_specs=(
            P("pop", None, "tp"),
            P("pop", None, "tp"),
            P("pop", None, "tp"),
            P("pop", None, "tp"),
            P("pop", "tp"),
            P("pop", None),
            P("pop", "tp"),
            P("pop"),
            P("pop"),
        ),
        out_specs=(P("pop", None, "tp"), P("pop", "tp")),
        check_vma=False,
    )
```

```python
import functools
import math

import jax
import jax.numpy as jnp
from jax import lax
from jax.experimental import pallas as pl
from jax.experimental.pallas import tpu as pltpu
from jax.sharding import PartitionSpec as P

HEAD = 64
SIGMA = 0.5
LANES = 128
WCUTS = 4
TCUTS = 2
MESH = pl.DeviceIdType.MESH
F32 = jnp.float32
BF16 = jnp.bfloat16


def dot_nt(a, b):
    return lax.dot_general(a, b, (((1,), (1,)), ((), ())), preferred_element_type=F32)


def dot_nn(a, b):
    return jnp.dot(a, b, preferred_element_type=F32)


def flip(index, bit):
    return index + bit - 2 * bit * lax.rem(lax.div(index, bit), 2)


def kernel(
    pop,
    tp,
    tok,
    rec_hbm,
    key_hbm,
    dec_hbm,
    w,
    nin_hbm,
    nout_hbm,
    util,
    live,
    wkv_hbm,
    left_out,
    right_out,
    tok_buf,
    wbuf,
    rec,
    key,
    dec,
    nin,
    nout,
    acc,
    s_low,
    s_high,
    proj,
    small_src,
    small_dst,
    factor_buf,
    wkv,
    own_sem,
    wkv_sem,
    small_send,
    small_recv,
    group_send,
    group_recv,
    x_send,
    x_recv,
    y_send,
    y_recv,
    c_send,
    c_recv,
    dn_send,
    dn_recv,
    up_send,
    up_recv,
):
    length, width = rec.shape[1], rec.shape[2]
    full = tp * width
    rows = w.shape[0]
    group = pop // 8
    block = rows * group
    cut = block // WCUTS
    tcut = length // TCUTS
    win = factor_buf.shape[0]
    half = length // 2

    p = lax.axis_index("pop")
    k = lax.axis_index("tp")
    q = lax.div(p, group)
    place = lax.rem(p, group)

    def remote(src, dst, send, recv, **where):
        return pltpu.make_async_remote_copy(
            src_ref=src, dst_ref=dst, send_sem=send, recv_sem=recv, device_id=where, device_id_type=MESH
        )

    barrier = pltpu.get_barrier_semaphore()
    for d in range(1, pop):
        pl.semaphore_signal(barrier, inc=1, device_id={"pop": lax.rem(p + d, pop)}, device_id_type=MESH)

    @pl.when(k >= 1)
    def _():
        pl.semaphore_signal(barrier, inc=1, device_id={"tp": k - 1}, device_id_type=MESH)

    @pl.when(k <= tp - 2)
    def _():
        pl.semaphore_signal(barrier, inc=1, device_id={"tp": k + 1}, device_id_type=MESH)

    own_tok = pltpu.make_async_copy(tok.at[0], tok_buf.at[k], own_sem.at[0])
    own_w = pltpu.make_async_copy(w, wbuf.at[pl.ds(pl.multiple_of(p * rows, rows), rows)], own_sem.at[1])
    loads = [
        pltpu.make_async_copy(src, dst, own_sem.at[2 + i])
        for i, (src, dst) in enumerate(
            ((nin_hbm, nin), (nout_hbm, nout), (dec_hbm, dec), (rec_hbm, rec), (key_hbm, key))
        )
    ]
    for copy in loads:
        copy.start()
    own_tok.start()
    own_w.start()

    neighbours = jnp.where(k >= 1, 1, 0) + jnp.where(k <= tp - 2, 1, 0)
    pl.semaphore_wait(barrier, pop - 1 + neighbours)

    sent = []

    def tok_rows(index, c):
        return tok_buf.at[index, pl.ds(c * tcut, tcut)]

    def down(s, c):
        src = tok.at[0, pl.ds(c * tcut, tcut)] if s == 0 else tok_rows(k + s, c)
        return remote(src, tok_rows(k + s, c), dn_send.at[s, c], dn_recv.at[s, c], tp=k - 1)

    def up(s, c):
        src = tok.at[0, pl.ds(c * tcut, tcut)] if s == 0 else tok_rows(k - s, c)
        return remote(src, tok_rows(k - s, c), up_send.at[s, c], up_recv.at[s, c], tp=k + 1)

    def down_sends(s):
        return (k >= 1) & (k + s <= tp - 1)

    def up_sends(s):
        return (k <= tp - 2) & (k - s >= 0)

    def start_tokens(s, c):
        @pl.when(down_sends(s))
        def _():
            down(s, c).start()

        @pl.when(up_sends(s))
        def _():
            up(s, c).start()

    def take_tokens(s, c):
        @pl.when(k + 1 + s <= tp - 1)
        def _():
            landed = tok_rows(k + 1 + s, c)
            remote(landed, landed, dn_send.at[s, c], dn_recv.at[s, c], tp=k).wait_recv()

        @pl.when(k - 1 - s >= 0)
        def _():
            landed = tok_rows(k - 1 - s, c)
            remote(landed, landed, up_send.at[s, c], up_recv.at[s, c], tp=k).wait_recv()

        if s + 1 <= tp - 2:
            start_tokens(s + 1, c)

    qx, qy, qc = flip(q, 2), flip(q, 4), flip(q, 1)
    qd = flip(qx, 4)

    def piece(index, c):
        return wbuf.at[pl.ds(pl.multiple_of(index * block + c * cut, cut), cut)]

    def own_piece(c):
        return w.at[pl.ds(c * cut, cut)] if group == 1 else piece(q, c)

    def send(src, dst, sems, recvs, slot, target):
        copy = remote(src, dst, sems.at[slot], recvs.at[slot], pop=target * group + place)
        copy.start()
        sent.append(copy)

    def landed(index, c, recvs, slot):
        here = piece(index, c)
        remote(here, here, x_send.at[0], recvs.at[slot], pop=p).wait_recv()

    start_tokens(0, 0)

    if group > 1:
        mine = wbuf.at[pl.ds(pl.multiple_of(p * rows, rows), rows)]
        for d in range(1, group):
            target = q * group + lax.rem(place + d, group)
            copy = remote(w, mine, group_send.at[d - 1], group_recv.at[d - 1], pop=target)
            copy.start()
            sent.append(copy)
        own_w.wait()
        for d in range(1, group):
            origin = q * group + lax.rem(place + group - d, group)
            here = wbuf.at[pl.ds(pl.multiple_of(origin * rows, rows), rows)]
            remote(here, here, group_send.at[d - 1], group_recv.at[d - 1], pop=p).wait_recv()

    x_order = list(range(WCUTS))
    y_order = x_order[WCUTS // 2 :] + x_order[: WCUTS // 2]
    def send_own(i):
        send(own_piece(x_order[i]), piece(q, x_order[i]), x_send, x_recv, x_order[i], qx)
        send(own_piece(y_order[i]), piece(q, y_order[i]), y_send, y_recv, y_order[i], qy)

    send_own(0)
    send_own(1)
    loads[0].wait()
    loads[1].wait()
    scale = util[0] * (1.0 / math.sqrt(pop))
    weighted = nin[...].astype(F32) * scale
    out_factor = nout[...].astype(F32)
    for dest in range(pop):
        start = dest * rows // LANES * LANES
        small_src[dest, :, 0:win] = weighted[:, start : start + win]
        small_src[dest, :, win : win + width] = out_factor
    for d in range(1, pop):
        target = lax.rem(p + d, pop)
        copy = remote(small_src.at[target], small_dst.at[p], small_send.at[d - 1], small_recv.at[d - 1], pop=target)
        copy.start()
        sent.append(copy)
    small_dst[p] = small_src[p]
    for copy in loads[2:]:
        copy.wait()

    def round_of(i):
        if i < WCUTS:
            cx, cy = x_order[i], y_order[i]
            landed(qx, cx, x_recv, cx)
            if i < WCUTS // 2:
                send(piece(qx, cx), piece(qx, cx), y_send, y_recv, WCUTS + i, qy)
            send(piece(qx, cx), piece(qx, cx), c_send, c_recv, WCUTS + cx, qc)
            landed(qy, cy, y_recv, cy)
            if i < WCUTS // 2:
                send(piece(qy, cy), piece(qy, cy), x_send, x_recv, WCUTS + i, qx)
            send(piece(qy, cy), piece(qy, cy), c_send, c_recv, 2 * WCUTS + cy, qc)
        else:
            cx, cy = y_order[i - WCUTS], x_order[i - WCUTS]
            landed(qd, cx, x_recv, i)
            send(piece(qd, cx), piece(qd, cx), c_send, c_recv, 3 * WCUTS + cx, qc)
            landed(qd, cy, y_recv, i)
            send(piece(qd, cy), piece(qd, cy), c_send, c_recv, 3 * WCUTS + cy, qc)

    live_count = live[0]
    lane = lax.broadcasted_iota(jnp.int32, (half, LANES), 1)
    first = (lane < HEAD).astype(F32)
    second = 1.0 - first
    row = lax.broadcasted_iota(jnp.int32, (half, LANES), 0)
    masks = []
    span = 32
    col = lax.broadcasted_iota(jnp.int32, (half, half), 1)
    prow = lax.broadcasted_iota(jnp.int32, (half, half), 0)
    row_block, col_block = lax.div(prow, span), lax.div(col, span)
    diag_mask = (row_block == col_block) & (col <= prow)
    near_mask = (lax.rem(row_block, 2) == 1) & (col_block == row_block - 1)
    far_mask = (row_block >= 2) & (col_block < 2)
    lower = (
        lax.broadcasted_iota(jnp.int32, (length, length), 0) >= lax.broadcasted_iota(jnp.int32, (length, length), 1)
    ).astype(BF16)

    def spread(cum, at, count):
        return jnp.concatenate([jnp.broadcast_to(cum[a : a + 1], (count, LANES)) for a in at], 0)

    def heads_of(queries):
        return jnp.concatenate([queries * first, queries * second], 0).astype(BF16)

    def scores_of(index):
        lanes = pl.ds(pl.multiple_of(index * LANES, LANES), LANES)
        t = lax.broadcasted_iota(jnp.int32, (length, LANES), 0)
        mask = (t < live_count).astype(F32)
        recept = rec[0, :, lanes].astype(F32) * mask
        keys = key[0, :, lanes].astype(F32) * mask
        decay = (dec[0, :, lanes].astype(F32) * mask).astype(BF16)
        cum = dot_nn(lower, decay)
        fade = jnp.exp(-jnp.abs(cum - cum[half - 1 : half]))
        cross = dot_nt(heads_of(recept[half:] * fade[half:]), (keys[:half] * fade[:half]).astype(BF16))
        far = jnp.exp(-jnp.abs(cum - spread(cum, (63, 191), half)))
        near = jnp.exp(-jnp.abs(cum - spread(cum, (31, 95, 159, 223), 64)))
        inner = cum - spread(cum, tuple(range(15, length, span)), span)
        grow, shrink = jnp.exp(inner), jnp.exp(-inner)
        out = []
        for h in range(2):
            part = slice(h * half, (h + 1) * half)
            r, kk = recept[part], keys[part]
            far_s = dot_nt(heads_of(r * far[part]), (kk * far[part]).astype(BF16))
            near_s = dot_nt(heads_of(r * near[part]), (kk * near[part]).astype(BF16))
            diag_s = dot_nt(heads_of(r * grow[part]), (kk * shrink[part]).astype(BF16))
            for a in range(2):
                sel = slice(a * half, (a + 1) * half)
                out.append(
                    jnp.where(
                        diag_mask, diag_s[sel], jnp.where(near_mask, near_s[sel], jnp.where(far_mask, far_s[sel], 0.0))
                    ).astype(BF16)
                )
        cross = cross.astype(BF16)
        s_low[index, :, 0:half] = out[0]
        s_low[index, :, half : 2 * half] = out[1]
        s_high[index, :, 0:half] = cross[:half]
        s_high[index, :, half : 2 * half] = out[2]
        s_high[index, :, 2 * half : 3 * half] = cross[half:]
        s_high[index, :, 3 * half : 4 * half] = out[3]

    pairs = width // LANES

    def score_pairs(begin, end):
        @pl.loop(begin // 2, end // 2)
        def _(index):
            scores_of(index * 2)
            scores_of(index * 2 + 1)

    def update_part():
        for d in range(1, pop):
            origin = lax.rem(p + pop - d, pop)
            here = small_dst.at[origin]
            remote(here, here, small_send.at[d - 1], small_recv.at[d - 1], pop=p).wait_recv()
        factor = jnp.concatenate([small_dst[m, :, 0:win] for m in range(pop)], 0)
        high = factor.astype(BF16).astype(F32)
        mid = (factor - high).astype(BF16).astype(F32)
        low = factor - high - mid
        factor_buf[...] = jnp.concatenate([high, mid, low], 0).T
        offset = pl.multiple_of(lax.rem(p * rows, LANES) if rows < LANES else 0, 8)
        left_out[...] = factor_buf[pl.ds(offset, rows), :].astype(BF16)
        right = jnp.concatenate([small_dst[m, :, win : win + width] for m in range(pop)], 0)
        right_out[...] = jnp.concatenate([right, right, right], 0).astype(BF16)

    tile = 2 * LANES
    qxc, qyc, qdc = flip(qx, 1), flip(qy, 1), flip(qd, 1)
    near_blocks = (q, qc, qx, qxc, qy, qyc)
    last_blocks = (qd, qdc)
    all_pieces = tuple(range(WCUTS))

    def distance(index):
        j = lax.div(index * block, width)
        return jnp.maximum(j - k, k - j)

    def is_far(index):
        return distance(index) >= tp - 1

    def multiply(index, pieces, begin, end):
        j = lax.div(index * block, width)
        base = lax.rem(index * block, width)
        if pieces == all_pieces:
            spans = [(0, block)]
        else:
            spans = [(c * cut, cut) for c in pieces]

        @pl.loop(0, width // tile)
        def _(n):
            lanes = pl.ds(pl.multiple_of(n * tile, tile), tile)
            left = [tok_buf[j, begin:end, pl.ds(pl.multiple_of(base + o, LANES), size)] for o, size in spans]
            right = [wbuf[pl.ds(pl.multiple_of(index * block + o, LANES), size), lanes] for o, size in spans]
            if len(spans) > 1:
                left, right = [jnp.concatenate(left, 1)], [jnp.concatenate(right, 0)]
            acc[begin:end, lanes] += dot_nn(left[0], right[0])

    def project(j):
        part = jnp.broadcast_to(nin[:, j * width : (j + 1) * width].astype(F32), (LANES, width)).astype(BF16)
        proj[...] += dot_nt(tok_buf[j], part)

    def arrived(index, b, pieces):
        for c in pieces:
            landed(index, c, c_recv, b * WCUTS + c)

    acc[...] = jnp.zeros_like(acc)
    proj[...] = jnp.zeros_like(proj)
    early = (x_order[0], y_order[0])
    late = (x_order[1], y_order[1])
    share = pairs // 4
    score_pairs(0, share)
    start_tokens(0, 1)
    send_own(2)
    for i in range(WCUTS):
        send(own_piece(i), piece(q, i), c_send, c_recv, i, qc)
    take_tokens(0, 0)
    round_of(0)
    round_of(1)
    send_own(3)
    take_tokens(0, 1)
    score_pairs(share, 3 * share)
    take_tokens(1, 0)
    take_tokens(1, 1)
    round_of(2)
    round_of(3)
    score_pairs(3 * share, pairs)
    update_part()

    own_tok.wait()
    if group == 1:
        own_w.wait()
    for b, index in enumerate((qc, qxc, qyc)):
        arrived(index, b, all_pieces)
    for index in near_blocks:

        @pl.when(jnp.logical_not(is_far(index)))
        def _():
            multiply(index, all_pieces, 0, length)

    for j in range(tp):

        @pl.when(jnp.maximum(j - k, k - j) < tp - 1)
        def _():
            project(j)

    round_of(4)
    take_tokens(2, 0)
    arrived(qdc, 3, early)
    for index in near_blocks:

        @pl.when(is_far(index))
        def _():
            multiply(index, all_pieces, 0, half)

    for index in last_blocks:

        @pl.when(is_far(index))
        def _():
            multiply(index, early, 0, half)

        @pl.when(jnp.logical_not(is_far(index)))
        def _():
            multiply(index, early, 0, length)

    round_of(5)
    take_tokens(2, 1)
    for index in near_blocks:

        @pl.when(is_far(index))
        def _():
            multiply(index, all_pieces, half, length)

    for j in range(tp):

        @pl.when(jnp.maximum(j - k, k - j) >= tp - 1)
        def _():
            project(j)

    arrived(qdc, 3, late)
    for index in last_blocks:

        @pl.when(is_far(index))
        def _():
            multiply(index, late, 0, half)
            multiply(index, all_pieces, half, length)

        @pl.when(jnp.logical_not(is_far(index)))
        def _():
            multiply(index, late, 0, length)

    factor = proj[...] * (SIGMA / math.sqrt(full))

    @pl.loop(0, width // tile)
    def _(n):
        lanes = pl.ds(pl.multiple_of(n * tile, tile), tile)
        base = acc[:, lanes] + jnp.concatenate([factor, factor], 1) * nout[:, lanes].astype(F32)
        values = base.astype(BF16)
        for b in range(2):
            pair = values[:, b * LANES : (b + 1) * LANES].astype(F32)
            head_a = jnp.concatenate([pair[:half] * first, pair[half:] * first], 0).astype(BF16)
            head_b = jnp.concatenate([pair[:half] * second, pair[half:] * second], 0).astype(BF16)
            index = n * 2 + b
            low_v = jnp.concatenate([head_a[:half], head_b[:half]], 0)
            high_v = jnp.concatenate([head_a, head_b], 0)
            here = pl.ds(pl.multiple_of(index * LANES, LANES), LANES)
            wkv[0, 0:half, here] = dot_nn(s_low[index], low_v).astype(BF16)
            wkv[0, half:length, here] = dot_nn(s_high[index], high_v).astype(BF16)

    wkv_copy = pltpu.make_async_copy(wkv, wkv_hbm, wkv_sem)
    wkv_copy.start()
    for copy in sent:
        copy.wait_send()
    for s in range(tp - 1):
        for c in range(TCUTS):

            @pl.when(down_sends(s))
            def _():
                down(s, c).wait_send()

            @pl.when(up_sends(s))
            def _():
                up(s, c).wait_send()

    wkv_copy.wait()


def finish(wkv_in, left, right, wkv, upd, upd_buf, sems, wkv_sem):
    copy = pltpu.make_async_copy(wkv_in, wkv, wkv_sem)
    copy.start()
    count = sems.shape[0]
    size = upd_buf.shape[0] // count
    copies = []
    for i in range(count):
        here = slice(i * size, (i + 1) * size)
        upd_buf[here, :] = dot_nn(left[here, :], right[...])
        out = pltpu.make_async_copy(upd_buf.at[pl.ds(i * size, size)], upd.at[pl.ds(i * size, size)], sems.at[i])
        out.start()
        copies.append(out)
    for out in copies:
        out.wait()
    copy.wait()


def body(pop, tp, tokens, receptance, keys, log_decay, value_weight, noise_in, noise_out, utilities, live_length):
    length, width = receptance.shape[1:]
    rows = value_weight.shape[0]
    full = rows * pop
    win = max(rows, LANES)
    pairs = width // LANES
    half = length // 2
    group = pop // 8
    dma = pltpu.SemaphoreType.DMA
    whole = pl.BlockSpec(memory_space=pltpu.VMEM)
    scalar = pl.BlockSpec(memory_space=pltpu.SMEM)
    anywhere = pl.BlockSpec(memory_space=pl.ANY)
    hbm = pl.BlockSpec(memory_space=pltpu.HBM)
    wkv, left, right = pl.pallas_call(
        functools.partial(kernel, pop, tp),
        out_shape=(
            jax.ShapeDtypeStruct((1, length, width), BF16),
            jax.ShapeDtypeStruct((rows, 3 * pop), BF16),
            jax.ShapeDtypeStruct((3 * pop, width), BF16),
        ),
        in_specs=[hbm] * 7 + [scalar] * 2,
        out_specs=(anywhere, whole, whole),
        scratch_shapes=[
            pltpu.VMEM((tp, length, width), BF16),
            pltpu.VMEM((full, width), BF16),
            pltpu.VMEM((1, length, width), BF16),
            pltpu.VMEM((1, length, width), BF16),
            pltpu.VMEM((1, length, width), BF16),
            pltpu.VMEM((1, full), BF16),
            pltpu.VMEM((1, width), BF16),
            pltpu.VMEM((length, width), F32),
            pltpu.VMEM((pairs, half, 2 * half), BF16),
            pltpu.VMEM((pairs, half, 4 * half), BF16),
            pltpu.VMEM((length, LANES), F32),
            pltpu.VMEM((pop, 1, win + width), F32),
            pltpu.VMEM((pop, 1, win + width), F32),
            pltpu.VMEM((win, 3 * pop), F32),
            pltpu.VMEM((1, length, width), BF16),
            dma((7,)),
            dma,
            dma((pop - 1,)),
            dma((pop - 1,)),
            dma((max(group - 1, 1),)),
            dma((max(group - 1, 1),)),
            dma((2 * WCUTS,)),
            dma((2 * WCUTS,)),
            dma((2 * WCUTS,)),
            dma((2 * WCUTS,)),
            dma((4 * WCUTS,)),
            dma((4 * WCUTS,)),
            dma((tp - 1, TCUTS)),
            dma((tp - 1, TCUTS)),
            dma((tp - 1, TCUTS)),
            dma((tp - 1, TCUTS)),
        ],
        compiler_params=pltpu.CompilerParams(
            collective_id=0, has_side_effects=True, vmem_limit_bytes=63 * 1024 * 1024
        ),
        cost_estimate=pl.CostEstimate(
            flops=2 * length * full * width, bytes_accessed=16 * 1024 * 1024, transcendentals=5 * length * width
        ),
    )(tokens, receptance, keys, log_decay, value_weight, noise_in, noise_out, utilities, live_length)
    tiles = max(rows // LANES, 1)
    return pl.pallas_call(
        finish,
        out_shape=(
            jax.ShapeDtypeStruct((1, length, width), BF16),
            jax.ShapeDtypeStruct((rows, width), F32),
        ),
        in_specs=[anywhere, whole, whole],
        out_specs=(anywhere, anywhere),
        scratch_shapes=[pltpu.VMEM((rows, width), F32), dma((tiles,)), dma],
        compiler_params=pltpu.CompilerParams(vmem_limit_bytes=63 * 1024 * 1024),
    )(wkv, left, right)


def solution(mesh):
    return jax.shard_map(
        functools.partial(body, mesh.shape["pop"], mesh.shape["tp"]),
        mesh=mesh,
        in_specs=(
            P("pop", None, "tp"),
            P("pop", None, "tp"),
            P("pop", None, "tp"),
            P("pop", None, "tp"),
            P("pop", "tp"),
            P("pop", None),
            P("pop", "tp"),
            P("pop"),
            P("pop"),
        ),
        out_specs=(P("pop", None, "tp"), P("pop", "tp")),
        check_vma=False,
    )
```

```python
import functools
import math

import jax
import jax.numpy as jnp
from jax import lax
from jax.experimental import pallas as pl
from jax.experimental.pallas import tpu as pltpu
from jax.sharding import PartitionSpec as P

HEAD = 64
SIGMA = 0.5
LANES = 128
WCUTS = 4
TCUTS = 2
MESH = pl.DeviceIdType.MESH
F32 = jnp.float32
BF16 = jnp.bfloat16


def dot_nt(a, b):
    return lax.dot_general(a, b, (((1,), (1,)), ((), ())), preferred_element_type=F32)


def dot_nn(a, b):
    return jnp.dot(a, b, preferred_element_type=F32)


def flip(index, bit):
    return index + bit - 2 * bit * lax.rem(lax.div(index, bit), 2)


def kernel(
    pop,
    tp,
    tok,
    rec_hbm,
    key_hbm,
    dec_hbm,
    w,
    nin_hbm,
    nout_hbm,
    util,
    live,
    wkv_hbm,
    left_out,
    right_out,
    tok_buf,
    wbuf,
    rec,
    key,
    dec,
    nin,
    nout,
    acc,
    s_low,
    s_high,
    proj,
    small_src,
    small_dst,
    factor_buf,
    wkv,
    own_sem,
    wkv_sem,
    small_send,
    small_recv,
    group_send,
    group_recv,
    x_send,
    x_recv,
    y_send,
    y_recv,
    c_send,
    c_recv,
    dn_send,
    dn_recv,
    up_send,
    up_recv,
):
    length, width = rec.shape[1], rec.shape[2]
    full = tp * width
    rows = w.shape[0]
    group = pop // 8
    block = rows * group
    cut = block // WCUTS
    tcut = length // TCUTS
    win = factor_buf.shape[0]
    half = length // 2

    p = lax.axis_index("pop")
    k = lax.axis_index("tp")
    q = lax.div(p, group)
    place = lax.rem(p, group)

    def remote(src, dst, send, recv, **where):
        return pltpu.make_async_remote_copy(
            src_ref=src, dst_ref=dst, send_sem=send, recv_sem=recv, device_id=where, device_id_type=MESH
        )

    barrier = pltpu.get_barrier_semaphore()
    for d in range(1, pop):
        pl.semaphore_signal(barrier, inc=1, device_id={"pop": lax.rem(p + d, pop)}, device_id_type=MESH)

    @pl.when(k >= 1)
    def _():
        pl.semaphore_signal(barrier, inc=1, device_id={"tp": k - 1}, device_id_type=MESH)

    @pl.when(k <= tp - 2)
    def _():
        pl.semaphore_signal(barrier, inc=1, device_id={"tp": k + 1}, device_id_type=MESH)

    own_tok = pltpu.make_async_copy(tok.at[0], tok_buf.at[k], own_sem.at[0])
    own_w = pltpu.make_async_copy(w, wbuf.at[pl.ds(pl.multiple_of(p * rows, rows), rows)], own_sem.at[1])
    loads = [
        pltpu.make_async_copy(src, dst, own_sem.at[2 + i])
        for i, (src, dst) in enumerate(
            ((nin_hbm, nin), (nout_hbm, nout), (dec_hbm, dec), (rec_hbm, rec), (key_hbm, key))
        )
    ]
    for copy in loads:
        copy.start()
    own_tok.start()
    own_w.start()

    neighbours = jnp.where(k >= 1, 1, 0) + jnp.where(k <= tp - 2, 1, 0)
    pl.semaphore_wait(barrier, pop - 1 + neighbours)

    sent = []

    def tok_rows(index, c):
        return tok_buf.at[index, pl.ds(c * tcut, tcut)]

    def down(s, c):
        src = tok.at[0, pl.ds(c * tcut, tcut)] if s == 0 else tok_rows(k + s, c)
        return remote(src, tok_rows(k + s, c), dn_send.at[s, c], dn_recv.at[s, c], tp=k - 1)

    def up(s, c):
        src = tok.at[0, pl.ds(c * tcut, tcut)] if s == 0 else tok_rows(k - s, c)
        return remote(src, tok_rows(k - s, c), up_send.at[s, c], up_recv.at[s, c], tp=k + 1)

    def down_sends(s):
        return (k >= 1) & (k + s <= tp - 1)

    def up_sends(s):
        return (k <= tp - 2) & (k - s >= 0)

    def start_tokens(s, c):
        @pl.when(down_sends(s))
        def _():
            down(s, c).start()

        @pl.when(up_sends(s))
        def _():
            up(s, c).start()

    def take_tokens(s, c):
        @pl.when(k + 1 + s <= tp - 1)
        def _():
            landed = tok_rows(k + 1 + s, c)
            remote(landed, landed, dn_send.at[s, c], dn_recv.at[s, c], tp=k).wait_recv()

        @pl.when(k - 1 - s >= 0)
        def _():
            landed = tok_rows(k - 1 - s, c)
            remote(landed, landed, up_send.at[s, c], up_recv.at[s, c], tp=k).wait_recv()

        if s + 1 <= tp - 2:
            start_tokens(s + 1, c)

    qx, qy, qc = flip(q, 2), flip(q, 4), flip(q, 1)
    qd = flip(qx, 4)

    def piece(index, c):
        return wbuf.at[pl.ds(pl.multiple_of(index * block + c * cut, cut), cut)]

    def own_piece(c):
        return w.at[pl.ds(c * cut, cut)] if group == 1 else piece(q, c)

    def send(src, dst, sems, recvs, slot, target):
        copy = remote(src, dst, sems.at[slot], recvs.at[slot], pop=target * group + place)
        copy.start()
        sent.append(copy)

    def landed(index, c, recvs, slot):
        here = piece(index, c)
        remote(here, here, x_send.at[0], recvs.at[slot], pop=p).wait_recv()

    start_tokens(0, 0)

    if group > 1:
        mine = wbuf.at[pl.ds(pl.multiple_of(p * rows, rows), rows)]
        for d in range(1, group):
            target = q * group + lax.rem(place + d, group)
            copy = remote(w, mine, group_send.at[d - 1], group_recv.at[d - 1], pop=target)
            copy.start()
            sent.append(copy)
        own_w.wait()
        for d in range(1, group):
            origin = q * group + lax.rem(place + group - d, group)
            here = wbuf.at[pl.ds(pl.multiple_of(origin * rows, rows), rows)]
            remote(here, here, group_send.at[d - 1], group_recv.at[d - 1], pop=p).wait_recv()

    x_order = list(range(WCUTS))
    y_order = x_order[WCUTS // 2 :] + x_order[: WCUTS // 2]
    def send_own(i):
        send(own_piece(x_order[i]), piece(q, x_order[i]), x_send, x_recv, x_order[i], qx)
        send(own_piece(y_order[i]), piece(q, y_order[i]), y_send, y_recv, y_order[i], qy)

    send_own(0)
    send_own(1)
    loads[0].wait()
    loads[1].wait()
    scale = util[0] * (1.0 / math.sqrt(pop))
    weighted = nin[...].astype(F32) * scale
    out_factor = nout[...].astype(F32)
    for dest in range(pop):
        start = dest * rows // LANES * LANES
        small_src[dest, :, 0:win] = weighted[:, start : start + win]
        small_src[dest, :, win : win + width] = out_factor
    for d in range(1, pop):
        target = lax.rem(p + d, pop)
        copy = remote(small_src.at[target], small_dst.at[p], small_send.at[d - 1], small_recv.at[d - 1], pop=target)
        copy.start()
        sent.append(copy)
    small_dst[p] = small_src[p]
    for copy in loads[2:]:
        copy.wait()

    def round_of(i):
        if i < WCUTS:
            cx, cy = x_order[i], y_order[i]
            landed(qx, cx, x_recv, cx)
            if i < WCUTS // 2:
                send(piece(qx, cx), piece(qx, cx), y_send, y_recv, WCUTS + i, qy)
            send(piece(qx, cx), piece(qx, cx), c_send, c_recv, WCUTS + cx, qc)
            landed(qy, cy, y_recv, cy)
            if i < WCUTS // 2:
                send(piece(qy, cy), piece(qy, cy), x_send, x_recv, WCUTS + i, qx)
            send(piece(qy, cy), piece(qy, cy), c_send, c_recv, 2 * WCUTS + cy, qc)
        else:
            cx, cy = y_order[i - WCUTS], x_order[i - WCUTS]
            landed(qd, cx, x_recv, i)
            send(piece(qd, cx), piece(qd, cx), c_send, c_recv, 3 * WCUTS + cx, qc)
            landed(qd, cy, y_recv, i)
            send(piece(qd, cy), piece(qd, cy), c_send, c_recv, 3 * WCUTS + cy, qc)

    live_count = live[0]
    quarter = length // 4
    wide = 2 * LANES
    lane = lax.broadcasted_iota(jnp.int32, (half, LANES), 1)
    first = (lane < HEAD).astype(BF16)
    second = (lane >= HEAD).astype(BF16)
    row = lax.broadcasted_iota(jnp.int32, (half, half), 0)
    col = lax.broadcasted_iota(jnp.int32, (half, half), 1)
    diag_mask = (col <= row) & ((row < quarter) | (col >= quarter))
    far_mask = lax.broadcasted_iota(jnp.int32, (quarter, half), 1) < quarter
    lower = (
        lax.broadcasted_iota(jnp.int32, (length, length), 0) >= lax.broadcasted_iota(jnp.int32, (length, length), 1)
    ).astype(BF16)

    def spread(cum, at, count):
        return jnp.concatenate([jnp.broadcast_to(cum[a : a + 1], (count, cum.shape[1])) for a in at], 0)

    def heads_of(queries):
        count = queries.shape[0]
        return jnp.concatenate([queries * first[:count], queries * second[:count]], 0)

    def scores_of(step):
        lanes = pl.ds(pl.multiple_of(step * wide, wide), wide)
        t = lax.broadcasted_iota(jnp.int32, (length, wide), 0)
        mask = (t < live_count).astype(F32)
        recept = rec[0, :, lanes].astype(F32) * mask
        keys = key[0, :, lanes].astype(F32) * mask
        cum = dot_nn(lower, dec[0, :, lanes] * mask.astype(BF16))
        fade = jnp.exp(-jnp.abs(cum - cum[half - 1 : half]))
        q_cross = (recept[half:] * fade[half:]).astype(BF16)
        k_cross = (keys[:half] * fade[:half]).astype(BF16)
        far = jnp.exp(-jnp.abs(cum - spread(cum, (quarter - 1, half + quarter - 1), half)))
        q_far = (recept * far).astype(BF16)
        k_far = (keys * far).astype(BF16)
        inner = cum - spread(cum, tuple(range(quarter // 2 - 1, length, quarter)), quarter)
        q_diag = (recept * jnp.exp(inner)).astype(BF16)
        k_diag = (keys * jnp.exp(-inner)).astype(BF16)
        for b in range(wide // LANES):
            index = step * (wide // LANES) + b
            part = slice(b * LANES, (b + 1) * LANES)
            cross = dot_nt(heads_of(q_cross[:, part]), k_cross[:, part]).astype(BF16)
            s_high[index, :, 0:half] = cross[:half]
            s_high[index, :, 2 * half : 3 * half] = cross[half:]
            for h in range(2):
                begin = h * half
                diag_s = dot_nt(heads_of(q_diag[begin : begin + half, part]), k_diag[begin : begin + half, part])
                far_s = dot_nt(
                    heads_of(q_far[begin + quarter : begin + half, part]), k_far[begin : begin + half, part]
                )
                for a in range(2):
                    own = jnp.where(diag_mask, diag_s[a * half : (a + 1) * half], 0.0)
                    low = jnp.where(far_mask, far_s[a * quarter : (a + 1) * quarter], own[quarter:])
                    if h == 0:
                        s_low[index, 0:quarter, a * half : (a + 1) * half] = own[:quarter].astype(BF16)
                        s_low[index, quarter:half, a * half : (a + 1) * half] = low.astype(BF16)
                    else:
                        at = (2 * a + 1) * half
                        s_high[index, 0:quarter, at : at + half] = own[:quarter].astype(BF16)
                        s_high[index, quarter:half, at : at + half] = low.astype(BF16)

    pairs = width // LANES

    def score_steps(begin, end):
        @pl.loop(begin, end)
        def _(step):
            scores_of(step)

    def update_part():
        for d in range(1, pop):
            origin = lax.rem(p + pop - d, pop)
            here = small_dst.at[origin]
            remote(here, here, small_send.at[d - 1], small_recv.at[d - 1], pop=p).wait_recv()
        factor = jnp.concatenate([small_dst[m, :, 0:win] for m in range(pop)], 0)
        high = factor.astype(BF16).astype(F32)
        mid = (factor - high).astype(BF16).astype(F32)
        low = factor - high - mid
        factor_buf[...] = jnp.concatenate([high, mid, low], 0).T
        offset = pl.multiple_of(lax.rem(p * rows, LANES) if rows < LANES else 0, 8)
        left_out[...] = factor_buf[pl.ds(offset, rows), :].astype(BF16)
        right = jnp.concatenate([small_dst[m, :, win : win + width] for m in range(pop)], 0)
        right_out[...] = jnp.concatenate([right, right, right], 0).astype(BF16)

    tile = 2 * LANES
    qxc, qyc, qdc = flip(qx, 1), flip(qy, 1), flip(qd, 1)
    near_blocks = (q, qc, qx, qxc, qy, qyc)
    last_blocks = (qd, qdc)
    all_pieces = tuple(range(WCUTS))

    def distance(index):
        j = lax.div(index * block, width)
        return jnp.maximum(j - k, k - j)

    def is_far(index):
        return distance(index) >= tp - 1

    def multiply(index, pieces, begin, end):
        j = lax.div(index * block, width)
        base = lax.rem(index * block, width)
        if pieces == all_pieces:
            spans = [(0, block)]
        else:
            spans = [(c * cut, cut) for c in pieces]

        @pl.loop(0, width // tile)
        def _(n):
            lanes = pl.ds(pl.multiple_of(n * tile, tile), tile)
            left = [tok_buf[j, begin:end, pl.ds(pl.multiple_of(base + o, LANES), size)] for o, size in spans]
            right = [wbuf[pl.ds(pl.multiple_of(index * block + o, LANES), size), lanes] for o, size in spans]
            if len(spans) > 1:
                left, right = [jnp.concatenate(left, 1)], [jnp.concatenate(right, 0)]
            acc[begin:end, lanes] += dot_nn(left[0], right[0])

    def project(j):
        part = jnp.broadcast_to(nin[:, j * width : (j + 1) * width].astype(F32), (LANES, width)).astype(BF16)
        proj[...] += dot_nt(tok_buf[j], part)

    def arrived(index, b, pieces):
        for c in pieces:
            landed(index, c, c_recv, b * WCUTS + c)

    acc[...] = jnp.zeros_like(acc)
    proj[...] = jnp.zeros_like(proj)
    early = (x_order[0], y_order[0])
    late = (x_order[1], y_order[1])
    steps = width // wide
    share = steps // 4
    start_tokens(0, 1)
    for i in range(WCUTS):
        send(own_piece(i), piece(q, i), c_send, c_recv, i, qc)
    score_steps(0, share)
    send_own(2)
    send_own(3)
    score_steps(share, 2 * share)
    take_tokens(0, 0)
    take_tokens(0, 1)
    round_of(0)
    round_of(1)
    score_steps(2 * share, steps)
    take_tokens(1, 0)
    take_tokens(1, 1)
    round_of(2)
    round_of(3)
    update_part()

    own_tok.wait()
    if group == 1:
        own_w.wait()
    for b, index in enumerate((qc, qxc, qyc)):
        arrived(index, b, all_pieces)
    for index in near_blocks:

        @pl.when(jnp.logical_not(is_far(index)))
        def _():
            multiply(index, all_pieces, 0, length)

    for j in range(tp):

        @pl.when(jnp.maximum(j - k, k - j) < tp - 1)
        def _():
            project(j)

    round_of(4)
    take_tokens(2, 0)
    arrived(qdc, 3, early)
    for index in near_blocks:

        @pl.when(is_far(index))
        def _():
            multiply(index, all_pieces, 0, half)

    for index in last_blocks:

        @pl.when(is_far(index))
        def _():
            multiply(index, early, 0, half)

        @pl.when(jnp.logical_not(is_far(index)))
        def _():
            multiply(index, early, 0, length)

    round_of(5)
    take_tokens(2, 1)
    for index in near_blocks:

        @pl.when(is_far(index))
        def _():
            multiply(index, all_pieces, half, length)

    for j in range(tp):

        @pl.when(jnp.maximum(j - k, k - j) >= tp - 1)
        def _():
            project(j)

    arrived(qdc, 3, late)
    for index in last_blocks:

        @pl.when(is_far(index))
        def _():
            multiply(index, late, 0, half)
            multiply(index, all_pieces, half, length)

        @pl.when(jnp.logical_not(is_far(index)))
        def _():
            multiply(index, late, 0, length)

    factor = proj[...] * (SIGMA / math.sqrt(full))

    @pl.loop(0, width // tile)
    def _(n):
        lanes = pl.ds(pl.multiple_of(n * tile, tile), tile)
        base = acc[:, lanes] + jnp.concatenate([factor, factor], 1) * nout[:, lanes].astype(F32)
        values = base.astype(BF16)
        for b in range(2):
            pair = values[:, b * LANES : (b + 1) * LANES]
            head_a = jnp.concatenate([pair[:half] * first, pair[half:] * first], 0)
            head_b = jnp.concatenate([pair[:half] * second, pair[half:] * second], 0)
            index = n * 2 + b
            low_v = jnp.concatenate([head_a[:half], head_b[:half]], 0)
            high_v = jnp.concatenate([head_a, head_b], 0)
            here = pl.ds(pl.multiple_of(index * LANES, LANES), LANES)
            wkv[0, 0:half, here] = dot_nn(s_low[index], low_v).astype(BF16)
            wkv[0, half:length, here] = dot_nn(s_high[index], high_v).astype(BF16)

    wkv_copy = pltpu.make_async_copy(wkv, wkv_hbm, wkv_sem)
    wkv_copy.start()
    for copy in sent:
        copy.wait_send()
    for s in range(tp - 1):
        for c in range(TCUTS):

            @pl.when(down_sends(s))
            def _():
                down(s, c).wait_send()

            @pl.when(up_sends(s))
            def _():
                up(s, c).wait_send()

    wkv_copy.wait()


def finish(wkv_in, left, right, wkv, upd, upd_buf, wkv_buf, sems, wkv_sem):
    fetch = pltpu.make_async_copy(wkv_in, wkv_buf, wkv_sem.at[0])
    fetch.start()
    count = sems.shape[0]
    size = upd_buf.shape[0] // count
    copies = []
    for i in range(count):
        here = slice(i * size, (i + 1) * size)
        upd_buf[here, :] = dot_nn(left[here, :], right[...])
        out = pltpu.make_async_copy(upd_buf.at[pl.ds(i * size, size)], upd.at[pl.ds(i * size, size)], sems.at[i])
        out.start()
        copies.append(out)
        if i == 0:
            fetch.wait()
            out = pltpu.make_async_copy(wkv_buf, wkv, wkv_sem.at[1])
            out.start()
            copies.append(out)
    for out in copies:
        out.wait()


def body(pop, tp, tokens, receptance, keys, log_decay, value_weight, noise_in, noise_out, utilities, live_length):
    length, width = receptance.shape[1:]
    rows = value_weight.shape[0]
    full = rows * pop
    win = max(rows, LANES)
    pairs = width // LANES
    half = length // 2
    group = pop // 8
    dma = pltpu.SemaphoreType.DMA
    whole = pl.BlockSpec(memory_space=pltpu.VMEM)
    scalar = pl.BlockSpec(memory_space=pltpu.SMEM)
    hbm = pl.BlockSpec(memory_space=pltpu.HBM)
    wkv, left, right = pl.pallas_call(
        functools.partial(kernel, pop, tp),
        out_shape=(
            jax.ShapeDtypeStruct((1, length, width), BF16),
            jax.ShapeDtypeStruct((rows, 3 * pop), BF16),
            jax.ShapeDtypeStruct((3 * pop, width), BF16),
        ),
        in_specs=[hbm] * 7 + [scalar] * 2,
        out_specs=(hbm, whole, whole),
        scratch_shapes=[
            pltpu.VMEM((tp, length, width), BF16),
            pltpu.VMEM((full, width), BF16),
            pltpu.VMEM((1, length, width), BF16),
            pltpu.VMEM((1, length, width), BF16),
            pltpu.VMEM((1, length, width), BF16),
            pltpu.VMEM((1, full), BF16),
            pltpu.VMEM((1, width), BF16),
            pltpu.VMEM((length, width), F32),
            pltpu.VMEM((pairs, half, 2 * half), BF16),
            pltpu.VMEM((pairs, half, 4 * half), BF16),
            pltpu.VMEM((length, LANES), F32),
            pltpu.VMEM((pop, 1, win + width), F32),
            pltpu.VMEM((pop, 1, win + width), F32),
            pltpu.VMEM((win, 3 * pop), F32),
            pltpu.VMEM((1, length, width), BF16),
            dma((7,)),
            dma,
            dma((pop - 1,)),
            dma((pop - 1,)),
            dma((max(group - 1, 1),)),
            dma((max(group - 1, 1),)),
            dma((2 * WCUTS,)),
            dma((2 * WCUTS,)),
            dma((2 * WCUTS,)),
            dma((2 * WCUTS,)),
            dma((4 * WCUTS,)),
            dma((4 * WCUTS,)),
            dma((tp - 1, TCUTS)),
            dma((tp - 1, TCUTS)),
            dma((tp - 1, TCUTS)),
            dma((tp - 1, TCUTS)),
        ],
        compiler_params=pltpu.CompilerParams(
            collective_id=0, has_side_effects=True, vmem_limit_bytes=63 * 1024 * 1024
        ),
        cost_estimate=pl.CostEstimate(
            flops=2 * length * full * width, bytes_accessed=16 * 1024 * 1024, transcendentals=5 * length * width
        ),
    )(tokens, receptance, keys, log_decay, value_weight, noise_in, noise_out, utilities, live_length)
    tiles = max(rows // LANES, 1)
    return pl.pallas_call(
        finish,
        out_shape=(
            jax.ShapeDtypeStruct((1, length, width), BF16),
            jax.ShapeDtypeStruct((rows, width), F32),
        ),
        in_specs=[hbm, whole, whole],
        out_specs=(hbm, hbm),
        scratch_shapes=[pltpu.VMEM((rows, width), F32), pltpu.VMEM((1, length, width), BF16), dma((tiles,)), dma((2,))],
        compiler_params=pltpu.CompilerParams(vmem_limit_bytes=63 * 1024 * 1024),
    )(wkv, left, right)


def solution(mesh):
    return jax.shard_map(
        functools.partial(body, mesh.shape["pop"], mesh.shape["tp"]),
        mesh=mesh,
        in_specs=(
            P("pop", None, "tp"),
            P("pop", None, "tp"),
            P("pop", None, "tp"),
            P("pop", None, "tp"),
            P("pop", "tp"),
            P("pop", None),
            P("pop", "tp"),
            P("pop"),
            P("pop"),
        ),
        out_specs=(P("pop", None, "tp"), P("pop", "tp")),
        check_vma=False,
    )
```

```python
import functools
import math

import jax
import jax.numpy as jnp
from jax import lax
from jax.experimental import pallas as pl
from jax.experimental.pallas import tpu as pltpu
from jax.sharding import PartitionSpec as P

HEAD = 64
SIGMA = 0.5
LANES = 128
WCUTS = 4
TCUTS = 2
MESH = pl.DeviceIdType.MESH
F32 = jnp.float32
BF16 = jnp.bfloat16


def dot_nt(a, b):
    return lax.dot_general(a, b, (((1,), (1,)), ((), ())), preferred_element_type=F32)


def dot_nn(a, b):
    return jnp.dot(a, b, preferred_element_type=F32)


def flip(index, bit):
    return index + bit - 2 * bit * lax.rem(lax.div(index, bit), 2)


def kernel(
    pop,
    tp,
    tok,
    rec_hbm,
    key_hbm,
    dec_hbm,
    w,
    nin_hbm,
    nout_hbm,
    util,
    live,
    wkv_hbm,
    left_out,
    right_out,
    tok_buf,
    wbuf,
    rec,
    key,
    dec,
    nin,
    nout,
    acc,
    s_low,
    s_high,
    proj,
    small_src,
    small_dst,
    factor_buf,
    wkv,
    left_buf,
    right_buf,
    own_sem,
    wkv_sem,
    pass_sem,
    small_send,
    small_recv,
    group_send,
    group_recv,
    x_send,
    x_recv,
    y_send,
    y_recv,
    c_send,
    c_recv,
    dn_send,
    dn_recv,
    up_send,
    up_recv,
):
    length, width = rec.shape[1], rec.shape[2]
    full = tp * width
    rows = w.shape[0]
    group = pop // 8
    block = rows * group
    cut = block // WCUTS
    tcut = length // TCUTS
    win = factor_buf.shape[0]
    half = length // 2

    p = lax.axis_index("pop")
    k = lax.axis_index("tp")
    q = lax.div(p, group)
    place = lax.rem(p, group)

    def remote(src, dst, send, recv, **where):
        return pltpu.make_async_remote_copy(
            src_ref=src, dst_ref=dst, send_sem=send, recv_sem=recv, device_id=where, device_id_type=MESH
        )

    barrier = pltpu.get_barrier_semaphore()
    for d in range(1, pop):
        pl.semaphore_signal(barrier, inc=1, device_id={"pop": lax.rem(p + d, pop)}, device_id_type=MESH)

    @pl.when(k >= 1)
    def _():
        pl.semaphore_signal(barrier, inc=1, device_id={"tp": k - 1}, device_id_type=MESH)

    @pl.when(k <= tp - 2)
    def _():
        pl.semaphore_signal(barrier, inc=1, device_id={"tp": k + 1}, device_id_type=MESH)

    own_tok = pltpu.make_async_copy(tok.at[0], tok_buf.at[k], own_sem.at[0])
    own_w = pltpu.make_async_copy(w, wbuf.at[pl.ds(pl.multiple_of(p * rows, rows), rows)], own_sem.at[1])
    loads = [
        pltpu.make_async_copy(src, dst, own_sem.at[2 + i])
        for i, (src, dst) in enumerate(
            ((nin_hbm, nin), (nout_hbm, nout), (dec_hbm, dec), (rec_hbm, rec), (key_hbm, key))
        )
    ]
    for copy in loads:
        copy.start()
    own_tok.start()
    own_w.start()

    neighbours = jnp.where(k >= 1, 1, 0) + jnp.where(k <= tp - 2, 1, 0)
    pl.semaphore_wait(barrier, pop - 1 + neighbours)

    sent = []

    def tok_rows(index, c):
        return tok_buf.at[index, pl.ds(c * tcut, tcut)]

    def down(s, c):
        src = tok.at[0, pl.ds(c * tcut, tcut)] if s == 0 else tok_rows(k + s, c)
        return remote(src, tok_rows(k + s, c), dn_send.at[s, c], dn_recv.at[s, c], tp=k - 1)

    def up(s, c):
        src = tok.at[0, pl.ds(c * tcut, tcut)] if s == 0 else tok_rows(k - s, c)
        return remote(src, tok_rows(k - s, c), up_send.at[s, c], up_recv.at[s, c], tp=k + 1)

    def down_sends(s):
        return (k >= 1) & (k + s <= tp - 1)

    def up_sends(s):
        return (k <= tp - 2) & (k - s >= 0)

    def start_tokens(s, c):
        @pl.when(down_sends(s))
        def _():
            down(s, c).start()

        @pl.when(up_sends(s))
        def _():
            up(s, c).start()

    def take_tokens(s, c):
        @pl.when(k + 1 + s <= tp - 1)
        def _():
            landed = tok_rows(k + 1 + s, c)
            remote(landed, landed, dn_send.at[s, c], dn_recv.at[s, c], tp=k).wait_recv()

        @pl.when(k - 1 - s >= 0)
        def _():
            landed = tok_rows(k - 1 - s, c)
            remote(landed, landed, up_send.at[s, c], up_recv.at[s, c], tp=k).wait_recv()

        if s + 1 <= tp - 2:
            start_tokens(s + 1, c)

    qx, qy, qc = flip(q, 2), flip(q, 4), flip(q, 1)
    qd = flip(qx, 4)

    def piece(index, c):
        return wbuf.at[pl.ds(pl.multiple_of(index * block + c * cut, cut), cut)]

    def own_piece(c):
        return w.at[pl.ds(c * cut, cut)] if group == 1 else piece(q, c)

    def send(src, dst, sems, recvs, slot, target):
        copy = remote(src, dst, sems.at[slot], recvs.at[slot], pop=target * group + place)
        copy.start()
        sent.append(copy)

    def landed(index, c, recvs, slot):
        here = piece(index, c)
        remote(here, here, x_send.at[0], recvs.at[slot], pop=p).wait_recv()

    start_tokens(0, 0)

    if group > 1:
        mine = wbuf.at[pl.ds(pl.multiple_of(p * rows, rows), rows)]
        for d in range(1, group):
            target = q * group + lax.rem(place + d, group)
            copy = remote(w, mine, group_send.at[d - 1], group_recv.at[d - 1], pop=target)
            copy.start()
            sent.append(copy)
        own_w.wait()
        for d in range(1, group):
            origin = q * group + lax.rem(place + group - d, group)
            here = wbuf.at[pl.ds(pl.multiple_of(origin * rows, rows), rows)]
            remote(here, here, group_send.at[d - 1], group_recv.at[d - 1], pop=p).wait_recv()

    x_order = list(range(WCUTS))
    y_order = x_order[WCUTS // 2 :] + x_order[: WCUTS // 2]
    def send_own(i):
        send(own_piece(x_order[i]), piece(q, x_order[i]), x_send, x_recv, x_order[i], qx)
        send(own_piece(y_order[i]), piece(q, y_order[i]), y_send, y_recv, y_order[i], qy)

    send_own(0)
    send_own(1)
    for copy in loads[:2]:
        copy.wait()
    scale = util[0] * (1.0 / math.sqrt(pop))
    weighted = nin[...].astype(F32) * scale
    out_factor = nout[...].astype(F32)
    for dest in range(pop):
        start = dest * rows // LANES * LANES
        small_src[dest, :, 0:win] = weighted[:, start : start + win]
        small_src[dest, :, win : win + width] = out_factor
    for d in range(1, pop):
        target = lax.rem(p + d, pop)
        copy = remote(small_src.at[target], small_dst.at[p], small_send.at[d - 1], small_recv.at[d - 1], pop=target)
        copy.start()
        sent.append(copy)
    small_dst[p] = small_src[p]
    for copy in loads[2:]:
        copy.wait()

    def round_of(i):
        if i < WCUTS:
            cx, cy = x_order[i], y_order[i]
            landed(qx, cx, x_recv, cx)
            if i < WCUTS // 2:
                send(piece(qx, cx), piece(qx, cx), y_send, y_recv, WCUTS + i, qy)
            send(piece(qx, cx), piece(qx, cx), c_send, c_recv, WCUTS + cx, qc)
            landed(qy, cy, y_recv, cy)
            if i < WCUTS // 2:
                send(piece(qy, cy), piece(qy, cy), x_send, x_recv, WCUTS + i, qx)
            send(piece(qy, cy), piece(qy, cy), c_send, c_recv, 2 * WCUTS + cy, qc)
        else:
            cx, cy = y_order[i - WCUTS], x_order[i - WCUTS]
            landed(qd, cx, x_recv, i)
            send(piece(qd, cx), piece(qd, cx), c_send, c_recv, 3 * WCUTS + cx, qc)
            landed(qd, cy, y_recv, i)
            send(piece(qd, cy), piece(qd, cy), c_send, c_recv, 3 * WCUTS + cy, qc)

    live_count = live[0]
    quarter = length // 4
    wide = 2 * LANES
    lane = lax.broadcasted_iota(jnp.int32, (half, LANES), 1)
    first = (lane < HEAD).astype(BF16)
    second = (lane >= HEAD).astype(BF16)
    row = lax.broadcasted_iota(jnp.int32, (half, half), 0)
    col = lax.broadcasted_iota(jnp.int32, (half, half), 1)
    diag_mask = (col <= row) & ((row < quarter) | (col >= quarter))
    far_mask = lax.broadcasted_iota(jnp.int32, (quarter, half), 1) < quarter
    lower = (
        lax.broadcasted_iota(jnp.int32, (length, length), 0) >= lax.broadcasted_iota(jnp.int32, (length, length), 1)
    ).astype(BF16)

    def spread(cum, at, count):
        return jnp.concatenate([jnp.broadcast_to(cum[a : a + 1], (count, cum.shape[1])) for a in at], 0)

    def heads_of(queries):
        count = queries.shape[0]
        return jnp.concatenate([queries * first[:count], queries * second[:count]], 0)

    def scores_of(step):
        lanes = pl.ds(pl.multiple_of(step * wide, wide), wide)
        t = lax.broadcasted_iota(jnp.int32, (length, wide), 0)
        mask = (t < live_count).astype(F32)
        recept = rec[0, :, lanes].astype(F32) * mask
        keys = key[0, :, lanes].astype(F32) * mask
        cum = dot_nn(lower, dec[0, :, lanes] * mask.astype(BF16))
        fade = jnp.exp(-jnp.abs(cum - cum[half - 1 : half]))
        q_cross = (recept[half:] * fade[half:]).astype(BF16)
        k_cross = (keys[:half] * fade[:half]).astype(BF16)
        far = jnp.exp(-jnp.abs(cum - spread(cum, (quarter - 1, half + quarter - 1), half)))
        q_far = (recept * far).astype(BF16)
        k_far = (keys * far).astype(BF16)
        inner = cum - spread(cum, tuple(range(quarter // 2 - 1, length, quarter)), quarter)
        q_diag = (recept * jnp.exp(inner)).astype(BF16)
        k_diag = (keys * jnp.exp(-inner)).astype(BF16)
        for b in range(wide // LANES):
            index = step * (wide // LANES) + b
            part = slice(b * LANES, (b + 1) * LANES)
            cross = dot_nt(heads_of(q_cross[:, part]), k_cross[:, part]).astype(BF16)
            s_high[index, :, 0:half] = cross[:half]
            s_high[index, :, 2 * half : 3 * half] = cross[half:]
            for h in range(2):
                begin = h * half
                diag_s = dot_nt(heads_of(q_diag[begin : begin + half, part]), k_diag[begin : begin + half, part])
                far_s = dot_nt(
                    heads_of(q_far[begin + quarter : begin + half, part]), k_far[begin : begin + half, part]
                )
                for a in range(2):
                    own = jnp.where(diag_mask, diag_s[a * half : (a + 1) * half], 0.0)
                    low = jnp.where(far_mask, far_s[a * quarter : (a + 1) * quarter], own[quarter:])
                    if h == 0:
                        s_low[index, 0:quarter, a * half : (a + 1) * half] = own[:quarter].astype(BF16)
                        s_low[index, quarter:half, a * half : (a + 1) * half] = low.astype(BF16)
                    else:
                        at = (2 * a + 1) * half
                        s_high[index, 0:quarter, at : at + half] = own[:quarter].astype(BF16)
                        s_high[index, quarter:half, at : at + half] = low.astype(BF16)

    pairs = width // LANES

    def score_steps(begin, end):
        @pl.loop(begin, end)
        def _(step):
            scores_of(step)

    factor_copies = [
        pltpu.make_async_copy(left_buf, left_out, pass_sem.at[0]),
        pltpu.make_async_copy(right_buf, right_out, pass_sem.at[1]),
    ]

    def update_part():
        for d in range(1, pop):
            origin = lax.rem(p + pop - d, pop)
            here = small_dst.at[origin]
            remote(here, here, small_send.at[d - 1], small_recv.at[d - 1], pop=p).wait_recv()
        factor = jnp.concatenate([small_dst[m, :, 0:win] for m in range(pop)], 0)
        high = factor.astype(BF16).astype(F32)
        mid = (factor - high).astype(BF16).astype(F32)
        low = factor - high - mid
        factor_buf[...] = jnp.concatenate([high, mid, low], 0).T
        offset = pl.multiple_of(lax.rem(p * rows, LANES) if rows < LANES else 0, 8)
        left_buf[...] = factor_buf[pl.ds(offset, rows), :].astype(BF16)
        right = jnp.concatenate([small_dst[m, :, win : win + width] for m in range(pop)], 0)
        right_buf[...] = jnp.concatenate([right, right, right], 0).astype(BF16)
        for copy in factor_copies:
            copy.start()

    tile = 2 * LANES
    qxc, qyc, qdc = flip(qx, 1), flip(qy, 1), flip(qd, 1)
    near_blocks = (q, qc, qx, qxc, qy, qyc)
    last_blocks = (qd, qdc)
    all_pieces = tuple(range(WCUTS))

    def distance(index):
        j = lax.div(index * block, width)
        return jnp.maximum(j - k, k - j)

    def is_far(index):
        return distance(index) >= tp - 1

    def multiply(index, pieces, begin, end):
        j = lax.div(index * block, width)
        base = lax.rem(index * block, width)
        if pieces == all_pieces:
            spans = [(0, block)]
        else:
            spans = [(c * cut, cut) for c in pieces]

        @pl.loop(0, width // tile)
        def _(n):
            lanes = pl.ds(pl.multiple_of(n * tile, tile), tile)
            left = [tok_buf[j, begin:end, pl.ds(pl.multiple_of(base + o, LANES), size)] for o, size in spans]
            right = [wbuf[pl.ds(pl.multiple_of(index * block + o, LANES), size), lanes] for o, size in spans]
            if len(spans) > 1:
                left, right = [jnp.concatenate(left, 1)], [jnp.concatenate(right, 0)]
            acc[begin:end, lanes] += dot_nn(left[0], right[0])

    def project(j):
        part = jnp.broadcast_to(nin[:, j * width : (j + 1) * width].astype(F32), (LANES, width)).astype(BF16)
        proj[...] += dot_nt(tok_buf[j], part)

    def arrived(index, b, pieces):
        for c in pieces:
            landed(index, c, c_recv, b * WCUTS + c)

    acc[...] = jnp.zeros_like(acc)
    proj[...] = jnp.zeros_like(proj)
    early = (x_order[0], y_order[0])
    late = (x_order[1], y_order[1])
    steps = width // wide
    share = steps // 4
    start_tokens(0, 1)
    for i in range(WCUTS):
        send(own_piece(i), piece(q, i), c_send, c_recv, i, qc)
    score_steps(0, share)
    send_own(2)
    send_own(3)
    score_steps(share, 2 * share)
    take_tokens(0, 0)
    take_tokens(0, 1)
    round_of(0)
    round_of(1)
    score_steps(2 * share, steps)
    take_tokens(1, 0)
    take_tokens(1, 1)
    round_of(2)
    round_of(3)
    update_part()

    own_tok.wait()
    if group == 1:
        own_w.wait()
    for b, index in enumerate((qc, qxc, qyc)):
        arrived(index, b, all_pieces)
    for index in near_blocks:

        @pl.when(jnp.logical_not(is_far(index)))
        def _():
            multiply(index, all_pieces, 0, length)

    for j in range(tp):

        @pl.when(jnp.maximum(j - k, k - j) < tp - 1)
        def _():
            project(j)

    round_of(4)
    take_tokens(2, 0)
    arrived(qdc, 3, early)
    for index in near_blocks:

        @pl.when(is_far(index))
        def _():
            multiply(index, all_pieces, 0, half)

    for index in last_blocks:

        @pl.when(is_far(index))
        def _():
            multiply(index, early, 0, half)

        @pl.when(jnp.logical_not(is_far(index)))
        def _():
            multiply(index, early, 0, length)

    round_of(5)
    take_tokens(2, 1)
    for index in near_blocks:

        @pl.when(is_far(index))
        def _():
            multiply(index, all_pieces, half, length)

    for j in range(tp):

        @pl.when(jnp.maximum(j - k, k - j) >= tp - 1)
        def _():
            project(j)

    arrived(qdc, 3, late)
    for index in last_blocks:

        @pl.when(is_far(index))
        def _():
            multiply(index, late, 0, half)
            multiply(index, all_pieces, half, length)

        @pl.when(jnp.logical_not(is_far(index)))
        def _():
            multiply(index, late, 0, length)

    factor = proj[...] * (SIGMA / math.sqrt(full))

    def readout_copy(n):
        lanes = pl.ds(pl.multiple_of(n * tile, tile), tile)
        return pltpu.make_async_copy(wkv.at[0, :, lanes], wkv_hbm.at[0, :, lanes], wkv_sem.at[n])

    @pl.loop(0, width // tile)
    def _(n):
        lanes = pl.ds(pl.multiple_of(n * tile, tile), tile)
        base = acc[:, lanes] + jnp.concatenate([factor, factor], 1) * nout[:, lanes].astype(F32)
        values = base.astype(BF16)
        for b in range(2):
            pair = values[:, b * LANES : (b + 1) * LANES]
            head_a = jnp.concatenate([pair[:half] * first, pair[half:] * first], 0)
            head_b = jnp.concatenate([pair[:half] * second, pair[half:] * second], 0)
            index = n * 2 + b
            low_v = jnp.concatenate([head_a[:half], head_b[:half]], 0)
            high_v = jnp.concatenate([head_a, head_b], 0)
            here = pl.ds(pl.multiple_of(index * LANES, LANES), LANES)
            wkv[0, 0:half, here] = dot_nn(s_low[index], low_v).astype(BF16)
            wkv[0, half:length, here] = dot_nn(s_high[index], high_v).astype(BF16)
        readout_copy(n).start()

    for copy in sent:
        copy.wait_send()
    for s in range(tp - 1):
        for c in range(TCUTS):

            @pl.when(down_sends(s))
            def _():
                down(s, c).wait_send()

            @pl.when(up_sends(s))
            def _():
                up(s, c).wait_send()

    for n in range(width // tile):
        readout_copy(n).wait()
    for copy in factor_copies:
        copy.wait()


def finish(wkv_in, left_in, right_in, wkv, upd, upd_buf, wkv_buf, left, right, sems, load_sem, wkv_sem):
    loads = [
        pltpu.make_async_copy(src, dst, load_sem.at[i])
        for i, (src, dst) in enumerate(((left_in, left), (right_in, right), (wkv_in, wkv_buf)))
    ]
    for copy in loads:
        copy.start()
    loads[0].wait()
    loads[1].wait()
    count = sems.shape[0]
    size = upd_buf.shape[0] // count
    copies = []
    for i in range(count):
        here = slice(i * size, (i + 1) * size)
        upd_buf[here, :] = dot_nn(left[here, :], right[...])
        out = pltpu.make_async_copy(upd_buf.at[pl.ds(i * size, size)], upd.at[pl.ds(i * size, size)], sems.at[i])
        out.start()
        copies.append(out)
        if i == 0:
            loads[2].wait()
            out = pltpu.make_async_copy(wkv_buf, wkv, wkv_sem)
            out.start()
            copies.append(out)
    for out in copies:
        out.wait()


def body(pop, tp, tokens, receptance, keys, log_decay, value_weight, noise_in, noise_out, utilities, live_length):
    length, width = receptance.shape[1:]
    rows = value_weight.shape[0]
    full = rows * pop
    win = max(rows, LANES)
    pairs = width // LANES
    half = length // 2
    group = pop // 8
    dma = pltpu.SemaphoreType.DMA
    hbm = pl.BlockSpec(memory_space=pltpu.HBM)
    scalar = pl.BlockSpec(memory_space=pltpu.SMEM)
    wkv, left, right = pl.pallas_call(
        functools.partial(kernel, pop, tp),
        out_shape=(
            jax.ShapeDtypeStruct((1, length, width), BF16),
            jax.ShapeDtypeStruct((rows, 3 * pop), BF16),
            jax.ShapeDtypeStruct((3 * pop, width), BF16),
        ),
        in_specs=[hbm] * 7 + [scalar] * 2,
        out_specs=(hbm, hbm, hbm),
        scratch_shapes=[
            pltpu.VMEM((tp, length, width), BF16),
            pltpu.VMEM((full, width), BF16),
            pltpu.VMEM((1, length, width), BF16),
            pltpu.VMEM((1, length, width), BF16),
            pltpu.VMEM((1, length, width), BF16),
            pltpu.VMEM((1, full), BF16),
            pltpu.VMEM((1, width), BF16),
            pltpu.VMEM((length, width), F32),
            pltpu.VMEM((pairs, half, 2 * half), BF16),
            pltpu.VMEM((pairs, half, 4 * half), BF16),
            pltpu.VMEM((length, LANES), F32),
            pltpu.VMEM((pop, 1, win + width), F32),
            pltpu.VMEM((pop, 1, win + width), F32),
            pltpu.VMEM((win, 3 * pop), F32),
            pltpu.VMEM((1, length, width), BF16),
            pltpu.VMEM((rows, 3 * pop), BF16),
            pltpu.VMEM((3 * pop, width), BF16),
            dma((7,)),
            dma((width // (2 * LANES),)),
            dma((2,)),
            dma((pop - 1,)),
            dma((pop - 1,)),
            dma((max(group - 1, 1),)),
            dma((max(group - 1, 1),)),
            dma((2 * WCUTS,)),
            dma((2 * WCUTS,)),
            dma((2 * WCUTS,)),
            dma((2 * WCUTS,)),
            dma((4 * WCUTS,)),
            dma((4 * WCUTS,)),
            dma((tp - 1, TCUTS)),
            dma((tp - 1, TCUTS)),
            dma((tp - 1, TCUTS)),
            dma((tp - 1, TCUTS)),
        ],
        compiler_params=pltpu.CompilerParams(
            collective_id=0, has_side_effects=True, vmem_limit_bytes=63 * 1024 * 1024
        ),
        cost_estimate=pl.CostEstimate(
            flops=2 * length * full * width, bytes_accessed=16 * 1024 * 1024, transcendentals=5 * length * width
        ),
    )(tokens, receptance, keys, log_decay, value_weight, noise_in, noise_out, utilities, live_length)
    tiles = max(rows // LANES, 1)
    return pl.pallas_call(
        finish,
        out_shape=(
            jax.ShapeDtypeStruct((1, length, width), BF16),
            jax.ShapeDtypeStruct((rows, width), F32),
        ),
        in_specs=[hbm] * 3,
        out_specs=(hbm, hbm),
        scratch_shapes=[
            pltpu.VMEM((rows, width), F32),
            pltpu.VMEM((1, length, width), BF16),
            pltpu.VMEM((rows, 3 * pop), BF16),
            pltpu.VMEM((3 * pop, width), BF16),
            dma((tiles,)),
            dma((3,)),
            dma,
        ],
        compiler_params=pltpu.CompilerParams(vmem_limit_bytes=63 * 1024 * 1024),
    )(wkv, left, right)


def solution(mesh):
    return jax.shard_map(
        functools.partial(body, mesh.shape["pop"], mesh.shape["tp"]),
        mesh=mesh,
        in_specs=(
            P("pop", None, "tp"),
            P("pop", None, "tp"),
            P("pop", None, "tp"),
            P("pop", None, "tp"),
            P("pop", "tp"),
            P("pop", None),
            P("pop", "tp"),
            P("pop"),
            P("pop"),
        ),
        out_specs=(P("pop", None, "tp"), P("pop", "tp")),
        check_vma=False,
    )
```

```python
import functools
import math

import jax
import jax.numpy as jnp
from jax import lax
from jax.experimental import pallas as pl
from jax.experimental.pallas import tpu as pltpu
from jax.sharding import PartitionSpec as P

HEAD = 64
SIGMA = 0.5
LANES = 128
WCUTS = 4
TCUTS = 2
MESH = pl.DeviceIdType.MESH
F32 = jnp.float32
BF16 = jnp.bfloat16


def dot_nt(a, b):
    return lax.dot_general(a, b, (((1,), (1,)), ((), ())), preferred_element_type=F32)


def dot_nn(a, b):
    return jnp.dot(a, b, preferred_element_type=F32)


def flip(index, bit):
    return index + bit - 2 * bit * lax.rem(lax.div(index, bit), 2)


def kernel(
    pop,
    tp,
    tok,
    rec_hbm,
    key_hbm,
    dec_hbm,
    w,
    nin_hbm,
    nout_hbm,
    util,
    live,
    wkv_hbm,
    left_out,
    right_out,
    tok_buf,
    wbuf,
    rec,
    key,
    dec,
    nin,
    nout,
    acc,
    s_low,
    s_high,
    proj,
    small_src,
    small_dst,
    factor_buf,
    wkv,
    left_buf,
    right_buf,
    own_sem,
    wkv_sem,
    pass_sem,
    small_send,
    small_recv,
    group_send,
    group_recv,
    x_send,
    x_recv,
    y_send,
    y_recv,
    c_send,
    c_recv,
    dn_send,
    dn_recv,
    up_send,
    up_recv,
):
    length, width = rec.shape[1], rec.shape[2]
    full = tp * width
    rows = w.shape[0]
    group = pop // 8
    block = rows * group
    cut = block // WCUTS
    tcut = length // TCUTS
    win = factor_buf.shape[0]
    half = length // 2

    p = lax.axis_index("pop")
    k = lax.axis_index("tp")
    q = lax.div(p, group)
    place = lax.rem(p, group)

    def remote(src, dst, send, recv, **where):
        return pltpu.make_async_remote_copy(
            src_ref=src, dst_ref=dst, send_sem=send, recv_sem=recv, device_id=where, device_id_type=MESH
        )

    barrier = pltpu.get_barrier_semaphore()
    for d in range(1, pop):
        pl.semaphore_signal(barrier, inc=1, device_id={"pop": lax.rem(p + d, pop)}, device_id_type=MESH)

    @pl.when(k >= 1)
    def _():
        pl.semaphore_signal(barrier, inc=1, device_id={"tp": k - 1}, device_id_type=MESH)

    @pl.when(k <= tp - 2)
    def _():
        pl.semaphore_signal(barrier, inc=1, device_id={"tp": k + 1}, device_id_type=MESH)

    own_tok = pltpu.make_async_copy(tok.at[0], tok_buf.at[k], own_sem.at[0])
    own_w = pltpu.make_async_copy(w, wbuf.at[pl.ds(pl.multiple_of(p * rows, rows), rows)], own_sem.at[1])
    loads = [
        pltpu.make_async_copy(src, dst, own_sem.at[2 + i])
        for i, (src, dst) in enumerate(
            ((nin_hbm, nin), (nout_hbm, nout), (dec_hbm, dec), (rec_hbm, rec), (key_hbm, key))
        )
    ]
    for copy in loads:
        copy.start()
    own_tok.start()
    own_w.start()

    neighbours = jnp.where(k >= 1, 1, 0) + jnp.where(k <= tp - 2, 1, 0)
    pl.semaphore_wait(barrier, pop - 1 + neighbours)

    sent = []

    def tok_rows(index, c):
        return tok_buf.at[index, pl.ds(c * tcut, tcut)]

    def down(s, c):
        src = tok.at[0, pl.ds(c * tcut, tcut)] if s == 0 else tok_rows(k + s, c)
        return remote(src, tok_rows(k + s, c), dn_send.at[s, c], dn_recv.at[s, c], tp=k - 1)

    def up(s, c):
        src = tok.at[0, pl.ds(c * tcut, tcut)] if s == 0 else tok_rows(k - s, c)
        return remote(src, tok_rows(k - s, c), up_send.at[s, c], up_recv.at[s, c], tp=k + 1)

    def down_sends(s):
        return (k >= 1) & (k + s <= tp - 1)

    def up_sends(s):
        return (k <= tp - 2) & (k - s >= 0)

    def start_tokens(s, c):
        @pl.when(down_sends(s))
        def _():
            down(s, c).start()

        @pl.when(up_sends(s))
        def _():
            up(s, c).start()

    def take_tokens(s, c):
        @pl.when(k + 1 + s <= tp - 1)
        def _():
            landed = tok_rows(k + 1 + s, c)
            remote(landed, landed, dn_send.at[s, c], dn_recv.at[s, c], tp=k).wait_recv()

        @pl.when(k - 1 - s >= 0)
        def _():
            landed = tok_rows(k - 1 - s, c)
            remote(landed, landed, up_send.at[s, c], up_recv.at[s, c], tp=k).wait_recv()

        if s + 1 <= tp - 2:
            start_tokens(s + 1, c)

    qx, qy, qc = flip(q, 2), flip(q, 4), flip(q, 1)
    qd = flip(qx, 4)

    def piece(index, c):
        return wbuf.at[pl.ds(pl.multiple_of(index * block + c * cut, cut), cut)]

    def own_piece(c):
        return w.at[pl.ds(c * cut, cut)] if group == 1 else piece(q, c)

    def send(src, dst, sems, recvs, slot, target):
        copy = remote(src, dst, sems.at[slot], recvs.at[slot], pop=target * group + place)
        copy.start()
        sent.append(copy)

    def landed(index, c, recvs, slot):
        here = piece(index, c)
        remote(here, here, x_send.at[0], recvs.at[slot], pop=p).wait_recv()

    start_tokens(0, 0)

    if group > 1:
        mine = wbuf.at[pl.ds(pl.multiple_of(p * rows, rows), rows)]
        for d in range(1, group):
            target = q * group + lax.rem(place + d, group)
            copy = remote(w, mine, group_send.at[d - 1], group_recv.at[d - 1], pop=target)
            copy.start()
            sent.append(copy)
        own_w.wait()
        for d in range(1, group):
            origin = q * group + lax.rem(place + group - d, group)
            here = wbuf.at[pl.ds(pl.multiple_of(origin * rows, rows), rows)]
            remote(here, here, group_send.at[d - 1], group_recv.at[d - 1], pop=p).wait_recv()

    x_order = list(range(WCUTS))
    y_order = x_order[WCUTS // 2 :] + x_order[: WCUTS // 2]
    def send_own(i):
        send(own_piece(x_order[i]), piece(q, x_order[i]), x_send, x_recv, x_order[i], qx)
        send(own_piece(y_order[i]), piece(q, y_order[i]), y_send, y_recv, y_order[i], qy)

    send_own(0)
    send_own(1)
    for copy in loads[:2]:
        copy.wait()
    scale = util[0] * (1.0 / math.sqrt(pop))
    weighted = nin[...].astype(F32) * scale
    out_factor = nout[...].astype(F32)
    for dest in range(pop):
        start = dest * rows // LANES * LANES
        small_src[dest, :, 0:win] = weighted[:, start : start + win]
        small_src[dest, :, win : win + width] = out_factor
    for d in range(1, pop):
        target = lax.rem(p + d, pop)
        copy = remote(small_src.at[target], small_dst.at[p], small_send.at[d - 1], small_recv.at[d - 1], pop=target)
        copy.start()
        sent.append(copy)
    small_dst[p] = small_src[p]
    for copy in loads[2:]:
        copy.wait()

    def round_of(i):
        if i < WCUTS:
            cx, cy = x_order[i], y_order[i]
            landed(qx, cx, x_recv, cx)
            if i < WCUTS // 2:
                send(piece(qx, cx), piece(qx, cx), y_send, y_recv, WCUTS + i, qy)
            send(piece(qx, cx), piece(qx, cx), c_send, c_recv, WCUTS + cx, qc)
            landed(qy, cy, y_recv, cy)
            if i < WCUTS // 2:
                send(piece(qy, cy), piece(qy, cy), x_send, x_recv, WCUTS + i, qx)
            send(piece(qy, cy), piece(qy, cy), c_send, c_recv, 2 * WCUTS + cy, qc)
        else:
            cx, cy = y_order[i - WCUTS], x_order[i - WCUTS]
            landed(qd, cx, x_recv, i)
            send(piece(qd, cx), piece(qd, cx), c_send, c_recv, 3 * WCUTS + cx, qc)
            landed(qd, cy, y_recv, i)
            send(piece(qd, cy), piece(qd, cy), c_send, c_recv, 3 * WCUTS + cy, qc)

    live_count = live[0]
    quarter = length // 4
    wide = 2 * LANES
    lane = lax.broadcasted_iota(jnp.int32, (half, LANES), 1)
    first = (lane < HEAD).astype(BF16)
    second = (lane >= HEAD).astype(BF16)
    row = lax.broadcasted_iota(jnp.int32, (half, half), 0)
    col = lax.broadcasted_iota(jnp.int32, (half, half), 1)
    diag_mask = (col <= row) & ((row < quarter) | (col >= quarter))
    far_mask = lax.broadcasted_iota(jnp.int32, (quarter, half), 1) < quarter
    lower = (
        lax.broadcasted_iota(jnp.int32, (length, length), 0) >= lax.broadcasted_iota(jnp.int32, (length, length), 1)
    ).astype(BF16)

    def spread(cum, at, count):
        return jnp.concatenate([jnp.broadcast_to(cum[a : a + 1], (count, cum.shape[1])) for a in at], 0)

    def heads_of(queries):
        count = queries.shape[0]
        return jnp.concatenate([queries * first[:count], queries * second[:count]], 0)

    def scores_of(step):
        lanes = pl.ds(pl.multiple_of(step * wide, wide), wide)
        t = lax.broadcasted_iota(jnp.int32, (length, wide), 0)
        mask = (t < live_count).astype(F32)
        recept = rec[0, :, lanes].astype(F32) * mask
        keys = key[0, :, lanes].astype(F32) * mask
        cum = dot_nn(lower, dec[0, :, lanes] * mask.astype(BF16))
        fade = jnp.exp(-jnp.abs(cum - cum[half - 1 : half]))
        q_cross = (recept[half:] * fade[half:]).astype(BF16)
        k_cross = (keys[:half] * fade[:half]).astype(BF16)
        far = jnp.exp(-jnp.abs(cum - spread(cum, (quarter - 1, half + quarter - 1), half)))
        q_far = (recept * far).astype(BF16)
        k_far = (keys * far).astype(BF16)
        inner = cum - spread(cum, tuple(range(quarter // 2 - 1, length, quarter)), quarter)
        q_diag = (recept * jnp.exp(inner)).astype(BF16)
        k_diag = (keys * jnp.exp(-inner)).astype(BF16)
        for b in range(wide // LANES):
            index = step * (wide // LANES) + b
            part = slice(b * LANES, (b + 1) * LANES)
            cross = dot_nt(heads_of(q_cross[:, part]), k_cross[:, part]).astype(BF16)
            s_high[index, :, 0:half] = cross[:half]
            s_high[index, :, 2 * half : 3 * half] = cross[half:]
            for h in range(2):
                begin = h * half
                diag_s = dot_nt(heads_of(q_diag[begin : begin + half, part]), k_diag[begin : begin + half, part])
                far_s = dot_nt(
                    heads_of(q_far[begin + quarter : begin + half, part]), k_far[begin : begin + half, part]
                )
                for a in range(2):
                    own = jnp.where(diag_mask, diag_s[a * half : (a + 1) * half], 0.0)
                    low = jnp.where(far_mask, far_s[a * quarter : (a + 1) * quarter], own[quarter:])
                    if h == 0:
                        s_low[index, 0:quarter, a * half : (a + 1) * half] = own[:quarter].astype(BF16)
                        s_low[index, quarter:half, a * half : (a + 1) * half] = low.astype(BF16)
                    else:
                        at = (2 * a + 1) * half
                        s_high[index, 0:quarter, at : at + half] = own[:quarter].astype(BF16)
                        s_high[index, quarter:half, at : at + half] = low.astype(BF16)

    pairs = width // LANES

    def score_steps(begin, end):
        @pl.loop(begin, end)
        def _(step):
            scores_of(step)

    factor_copies = [
        pltpu.make_async_copy(left_buf, left_out, pass_sem.at[0]),
        pltpu.make_async_copy(right_buf, right_out, pass_sem.at[1]),
    ]

    def update_part():
        for d in range(1, pop):
            origin = lax.rem(p + pop - d, pop)
            here = small_dst.at[origin]
            remote(here, here, small_send.at[d - 1], small_recv.at[d - 1], pop=p).wait_recv()
        factor = jnp.concatenate([small_dst[m, :, 0:win] for m in range(pop)], 0)
        high = factor.astype(BF16).astype(F32)
        mid = (factor - high).astype(BF16).astype(F32)
        low = factor - high - mid
        factor_buf[...] = jnp.concatenate([high, mid, low], 0).T
        offset = pl.multiple_of(lax.rem(p * rows, LANES) if rows < LANES else 0, 8)
        left_buf[...] = factor_buf[pl.ds(offset, rows), :].astype(BF16)
        right = jnp.concatenate([small_dst[m, :, win : win + width] for m in range(pop)], 0)
        right_buf[...] = jnp.concatenate([right, right, right], 0).astype(BF16)
        for copy in factor_copies:
            copy.start()

    tile = 2 * LANES
    qxc, qyc, qdc = flip(qx, 1), flip(qy, 1), flip(qd, 1)
    near_blocks = (q, qc, qx, qxc, qy, qyc)
    last_blocks = (qd, qdc)
    all_pieces = tuple(range(WCUTS))

    def distance(index):
        j = lax.div(index * block, width)
        return jnp.maximum(j - k, k - j)

    def is_far(index):
        return distance(index) >= tp - 1

    def multiply(index, pieces, begin, end):
        j = lax.div(index * block, width)
        base = lax.rem(index * block, width)
        if pieces == all_pieces:
            spans = [(0, block)]
        else:
            spans = [(c * cut, cut) for c in pieces]

        @pl.loop(0, width // tile)
        def _(n):
            lanes = pl.ds(pl.multiple_of(n * tile, tile), tile)
            left = [tok_buf[j, begin:end, pl.ds(pl.multiple_of(base + o, LANES), size)] for o, size in spans]
            right = [wbuf[pl.ds(pl.multiple_of(index * block + o, LANES), size), lanes] for o, size in spans]
            if len(spans) > 1:
                left, right = [jnp.concatenate(left, 1)], [jnp.concatenate(right, 0)]
            acc[begin:end, lanes] += dot_nn(left[0], right[0])

    def project(j):
        part = jnp.broadcast_to(nin[:, j * width : (j + 1) * width].astype(F32), (LANES, width)).astype(BF16)
        proj[...] += dot_nt(tok_buf[j], part)

    def arrived(index, b, pieces):
        for c in pieces:
            landed(index, c, c_recv, b * WCUTS + c)

    acc[...] = jnp.zeros_like(acc)
    proj[...] = jnp.zeros_like(proj)
    early = (x_order[0], y_order[0])
    late = (x_order[1], y_order[1])
    steps = width // wide
    share = steps // 4
    start_tokens(0, 1)
    for i in range(WCUTS):
        send(own_piece(i), piece(q, i), c_send, c_recv, i, qc)
    send_own(2)
    send_own(3)
    score_steps(0, 2 * share)
    take_tokens(0, 0)
    take_tokens(0, 1)
    round_of(0)
    round_of(1)
    score_steps(2 * share, steps)
    take_tokens(1, 0)
    take_tokens(1, 1)
    round_of(2)
    round_of(3)
    update_part()

    own_tok.wait()
    if group == 1:
        own_w.wait()
    for b, index in enumerate((qc, qxc, qyc)):
        arrived(index, b, all_pieces)
    for index in near_blocks:

        @pl.when(jnp.logical_not(is_far(index)))
        def _():
            multiply(index, all_pieces, 0, length)

    for j in range(tp):

        @pl.when(jnp.maximum(j - k, k - j) < tp - 1)
        def _():
            project(j)

    round_of(4)
    take_tokens(2, 0)
    arrived(qdc, 3, early)
    for index in near_blocks:

        @pl.when(is_far(index))
        def _():
            multiply(index, all_pieces, 0, half)

    for index in last_blocks:

        @pl.when(is_far(index))
        def _():
            multiply(index, early, 0, half)

        @pl.when(jnp.logical_not(is_far(index)))
        def _():
            multiply(index, early, 0, length)

    round_of(5)
    take_tokens(2, 1)
    for index in near_blocks:

        @pl.when(is_far(index))
        def _():
            multiply(index, all_pieces, half, length)

    for j in range(tp):

        @pl.when(jnp.maximum(j - k, k - j) >= tp - 1)
        def _():
            project(j)

    arrived(qdc, 3, late)
    for index in last_blocks:

        @pl.when(is_far(index))
        def _():
            multiply(index, late, 0, half)
            multiply(index, all_pieces, half, length)

        @pl.when(jnp.logical_not(is_far(index)))
        def _():
            multiply(index, late, 0, length)

    factor = proj[...] * (SIGMA / math.sqrt(full))

    def readout_copy(n):
        lanes = pl.ds(pl.multiple_of(n * tile, tile), tile)
        return pltpu.make_async_copy(wkv.at[0, :, lanes], wkv_hbm.at[0, :, lanes], wkv_sem.at[n])

    @pl.loop(0, width // tile)
    def _(n):
        lanes = pl.ds(pl.multiple_of(n * tile, tile), tile)
        base = acc[:, lanes] + jnp.concatenate([factor, factor], 1) * nout[:, lanes].astype(F32)
        values = base.astype(BF16)
        for b in range(2):
            pair = values[:, b * LANES : (b + 1) * LANES]
            head_a = jnp.concatenate([pair[:half] * first, pair[half:] * first], 0)
            head_b = jnp.concatenate([pair[:half] * second, pair[half:] * second], 0)
            index = n * 2 + b
            low_v = jnp.concatenate([head_a[:half], head_b[:half]], 0)
            high_v = jnp.concatenate([head_a, head_b], 0)
            here = pl.ds(pl.multiple_of(index * LANES, LANES), LANES)
            wkv[0, 0:half, here] = dot_nn(s_low[index], low_v).astype(BF16)
            wkv[0, half:length, here] = dot_nn(s_high[index], high_v).astype(BF16)
        readout_copy(n).start()

    for copy in sent:
        copy.wait_send()
    for s in range(tp - 1):
        for c in range(TCUTS):

            @pl.when(down_sends(s))
            def _():
                down(s, c).wait_send()

            @pl.when(up_sends(s))
            def _():
                up(s, c).wait_send()

    for n in range(width // tile):
        readout_copy(n).wait()
    for copy in factor_copies:
        copy.wait()


def finish(wkv_in, left_in, right_in, wkv, upd, upd_buf, wkv_buf, left, right, sems, load_sem, wkv_sem):
    loads = [
        pltpu.make_async_copy(src, dst, load_sem.at[i])
        for i, (src, dst) in enumerate(((left_in, left), (right_in, right), (wkv_in, wkv_buf)))
    ]
    for copy in loads:
        copy.start()
    loads[0].wait()
    loads[1].wait()
    count = sems.shape[0]
    size = upd_buf.shape[0] // count
    copies = []
    for i in range(count):
        here = slice(i * size, (i + 1) * size)
        upd_buf[here, :] = dot_nn(left[here, :], right[...])
        out = pltpu.make_async_copy(upd_buf.at[pl.ds(i * size, size)], upd.at[pl.ds(i * size, size)], sems.at[i])
        out.start()
        copies.append(out)
        if i == 0:
            loads[2].wait()
            out = pltpu.make_async_copy(wkv_buf, wkv, wkv_sem)
            out.start()
            copies.append(out)
    for out in copies:
        out.wait()


def body(pop, tp, tokens, receptance, keys, log_decay, value_weight, noise_in, noise_out, utilities, live_length):
    length, width = receptance.shape[1:]
    rows = value_weight.shape[0]
    full = rows * pop
    win = max(rows, LANES)
    pairs = width // LANES
    half = length // 2
    group = pop // 8
    dma = pltpu.SemaphoreType.DMA
    hbm = pl.BlockSpec(memory_space=pltpu.HBM)
    scalar = pl.BlockSpec(memory_space=pltpu.SMEM)
    wkv, left, right = pl.pallas_call(
        functools.partial(kernel, pop, tp),
        out_shape=(
            jax.ShapeDtypeStruct((1, length, width), BF16),
            jax.ShapeDtypeStruct((rows, 3 * pop), BF16),
            jax.ShapeDtypeStruct((3 * pop, width), BF16),
        ),
        in_specs=[hbm] * 7 + [scalar] * 2,
        out_specs=(hbm, hbm, hbm),
        scratch_shapes=[
            pltpu.VMEM((tp, length, width), BF16),
            pltpu.VMEM((full, width), BF16),
            pltpu.VMEM((1, length, width), BF16),
            pltpu.VMEM((1, length, width), BF16),
            pltpu.VMEM((1, length, width), BF16),
            pltpu.VMEM((1, full), BF16),
            pltpu.VMEM((1, width), BF16),
            pltpu.VMEM((length, width), F32),
            pltpu.VMEM((pairs, half, 2 * half), BF16),
            pltpu.VMEM((pairs, half, 4 * half), BF16),
            pltpu.VMEM((length, LANES), F32),
            pltpu.VMEM((pop, 1, win + width), F32),
            pltpu.VMEM((pop, 1, win + width), F32),
            pltpu.VMEM((win, 3 * pop), F32),
            pltpu.VMEM((1, length, width), BF16),
            pltpu.VMEM((rows, 3 * pop), BF16),
            pltpu.VMEM((3 * pop, width), BF16),
            dma((7,)),
            dma((width // (2 * LANES),)),
            dma((2,)),
            dma((pop - 1,)),
            dma((pop - 1,)),
            dma((max(group - 1, 1),)),
            dma((max(group - 1, 1),)),
            dma((2 * WCUTS,)),
            dma((2 * WCUTS,)),
            dma((2 * WCUTS,)),
            dma((2 * WCUTS,)),
            dma((4 * WCUTS,)),
            dma((4 * WCUTS,)),
            dma((tp - 1, TCUTS)),
            dma((tp - 1, TCUTS)),
            dma((tp - 1, TCUTS)),
            dma((tp - 1, TCUTS)),
        ],
        compiler_params=pltpu.CompilerParams(
            collective_id=0, has_side_effects=True, vmem_limit_bytes=63 * 1024 * 1024
        ),
        cost_estimate=pl.CostEstimate(
            flops=2 * length * full * width, bytes_accessed=16 * 1024 * 1024, transcendentals=5 * length * width
        ),
    )(tokens, receptance, keys, log_decay, value_weight, noise_in, noise_out, utilities, live_length)
    tiles = max(rows // LANES, 1)
    return pl.pallas_call(
        finish,
        out_shape=(
            jax.ShapeDtypeStruct((1, length, width), BF16),
            jax.ShapeDtypeStruct((rows, width), F32),
        ),
        in_specs=[hbm] * 3,
        out_specs=(hbm, hbm),
        scratch_shapes=[
            pltpu.VMEM((rows, width), F32),
            pltpu.VMEM((1, length, width), BF16),
            pltpu.VMEM((rows, 3 * pop), BF16),
            pltpu.VMEM((3 * pop, width), BF16),
            dma((tiles,)),
            dma((3,)),
            dma,
        ],
        compiler_params=pltpu.CompilerParams(vmem_limit_bytes=63 * 1024 * 1024),
    )(wkv, left, right)


def solution(mesh):
    return jax.shard_map(
        functools.partial(body, mesh.shape["pop"], mesh.shape["tp"]),
        mesh=mesh,
        in_specs=(
            P("pop", None, "tp"),
            P("pop", None, "tp"),
            P("pop", None, "tp"),
            P("pop", None, "tp"),
            P("pop", "tp"),
            P("pop", None),
            P("pop", "tp"),
            P("pop"),
            P("pop"),
        ),
        out_specs=(P("pop", None, "tp"), P("pop", "tp")),
        check_vma=False,
    )
```
